256 devices in a mesh: seq: 64 (over z, x, core), tp: 4 (over y).
Axes of the slice: x: 4, y: 4, z: 8, core: 2. Of those that a mesh axis runs over, the one named last changes fastest.
Arguments:
- tokens: bfloat16 [32768, 4096], P('seq', 'tp'), may hold values from -6 to 6
- log_decay: float32 [32768, 16], P('seq', 'tp'), may hold values from -2 to 0
- w_query: bfloat16 [4096, 2048], P(None, 'tp'), may hold values from -0.09375 to 0.09375
- w_key: bfloat16 [4096, 512], P(None, 'tp'), may hold values from -0.09375 to 0.09375
- w_value: bfloat16 [4096, 512], P(None, 'tp'), may hold values from -0.09375 to 0.09375
- w_level: bfloat16 [4096, 144], P(None, 'tp'), may hold values from -0.09375 to 0.09375
- w_out: bfloat16 [2048, 4096], P('tp'), may hold values from -0.125 to 0.125
Outputs:
- mixed: bfloat16 [32768, 4096], P('seq', 'tp')
The draws below stay inside these ranges and needn't reach their ends.
All inputs are finite; a program needn't handle non-finite values.
Results may differ from the reference program's by a relative error of at most 0.02.
Values may be sent and summed in bfloat16 or wider, within the bound.
A program may use at most 128 MiB of HBM per device.

```python
import jax
import jax.numpy as jnp
from jax import lax

D = 4096
HEAD_GROUP = 16
KV_HEADS = 4
DH = 128
BLOCK = 128
TOKEN_COUNT = 32768
LEVELS = 9
N_TP = 4


def draw_log_decay(key, part):
    key = jax.random.fold_in(key, 11)
    sequence_flows = jax.random.split(key, 7)
    slow_count = HEAD_GROUP // 2
    middle_count = HEAD_GROUP // 4
    ranking = jax.random.permutation(sequence_flows[0], HEAD_GROUP)
    fast_rate = jnp.exp(jax.random.uniform(sequence_flows[1], (HEAD_GROUP,), jnp.float32, jnp.log(1.0 / 50.0), jnp.log(1.0 / 30.0)))
    middle_rate = jnp.exp(jax.random.uniform(sequence_flows[6], (HEAD_GROUP,), jnp.float32, jnp.log(1.0 / 1000.0), jnp.log(1.0 / 200.0)))
    slow_rate = 0.3 / TOKEN_COUNT
    baseline_rate = jnp.where(ranking < slow_count, slow_rate, jnp.where(ranking < slow_count + middle_count, middle_rate, fast_rate))
    block_multiplier = jnp.exp(jax.random.uniform(sequence_flows[2], (TOKEN_COUNT // BLOCK, HEAD_GROUP), jnp.float32, -0.69, 0.69))
    block_multiplier = jnp.repeat(block_multiplier, BLOCK, axis=0, total_repeat_length=TOKEN_COUNT)
    random_offset = jax.random.uniform(sequence_flows[3], (TOKEN_COUNT, HEAD_GROUP), jnp.float32, 0.7, 1.3)
    spike_positions = jax.random.randint(sequence_flows[4], (2, HEAD_GROUP), 0, TOKEN_COUNT)
    spike_lengths = jax.random.uniform(sequence_flows[5], (2, HEAD_GROUP), jnp.float32, jnp.log(0.6), jnp.log(0.8))
    token_positions = jnp.arange(TOKEN_COUNT)[:, None]
    spike_runs = jnp.where(token_positions == spike_positions[0][None, :], spike_lengths[0][None, :], 0.0)
    spike_runs = spike_runs + jnp.where(token_positions == spike_positions[1][None, :], spike_lengths[1][None, :], 0.0)
    return (spike_runs - baseline_rate[None, :] * block_multiplier * random_offset).astype(jnp.float32)


def levels(rng, dims, pieces, low, top_value):
    level = 1.0
    for position, shards_of in pieces:
        draws = jax.random.uniform(jax.random.fold_in(jax.random.fold_in(rng, 6), position), (shards_of,), jnp.float32, low / len(pieces), top_value / len(pieces))
        level = level * jnp.repeat(jnp.exp(draws), dims[position] // shards_of).reshape((-1,) + (1,) * (len(dims) - 1 - position))
    return level


def bell_draw(stream_key, shape, deviation, bound, pieces=(), held_as=jnp.bfloat16):
    entries = deviation * jax.random.normal(stream_key, shape, jnp.float32)
    if pieces:
        entries = entries * levels(stream_key, shape, pieces, -0.22, 0.18)
    return jnp.clip(entries, -bound, bound).astype(held_as)


def setup_inputs(seed: int = 0) -> dict:
    key_of = jax.random.split(jax.random.key(seed), 8)
    tokens = bell_draw(key_of[0], (TOKEN_COUNT, D), 1.0, 6.0, ((0, 64), (1, 4)))
    log_decay = draw_log_decay(jax.random.fold_in(key_of[7], 71), 0)
    w_query = bell_draw(key_of[2], (D, HEAD_GROUP * DH), D ** -0.5, 0.09375, ((1, 4),))
    w_key = bell_draw(key_of[3], (D, KV_HEADS * DH), D ** -0.5, 0.09375, ((1, 4),))
    w_value = bell_draw(key_of[4], (D, KV_HEADS * DH), D ** -0.5, 0.09375, ((1, 4),))
    w_level = bell_draw(key_of[5], (D, HEAD_GROUP * LEVELS), D ** -0.5, 0.09375, ((1, 4),))
    w_out = bell_draw(key_of[6], (HEAD_GROUP * DH, D), (HEAD_GROUP * DH) ** -0.5, 0.125, ((0, 4),))
    return {"tokens": tokens, "log_decay": log_decay, "w_query": w_query, "w_key": w_key, "w_value": w_value, "w_level": w_level, "w_out": w_out}


def head_output(inputs):
    query, keys, values, weights, decay = inputs
    count = TOKEN_COUNT // BLOCK
    highest = lax.Precision.HIGHEST
    query_blocks = query.astype(jnp.float32).reshape(count, BLOCK, DH)
    key_blocks = keys.astype(jnp.float32).reshape(count, BLOCK, DH)
    value_blocks = values.astype(jnp.float32).reshape(count, BLOCK, DH)
    decay_blocks = decay.reshape(count, BLOCK)
    level_blocks = weights.reshape(count, BLOCK, LEVELS)
    inside = jnp.arange(BLOCK, dtype=jnp.int32)
    causal = inside[:, None] >= inside[None, :]
    scores = jnp.einsum('cik,cjk->cij', query_blocks, key_blocks, precision=highest)
    gaps = jnp.where(causal[None], decay_blocks[:, :, None] - decay_blocks[:, None, :], -jnp.inf)
    mixing = level_blocks[:, :, 0:1] * jnp.exp(gaps) * scores
    result = jnp.einsum('cij,cjv->civ', mixing, value_blocks, precision=highest)
    block_ends = decay_blocks[:, BLOCK - 1]
    weighted_keys = jnp.exp(block_ends[:, None] - decay_blocks)[:, :, None] * key_blocks
    block_states = jnp.einsum('cjk,cjv->ckv', weighted_keys, value_blocks, precision=highest)
    block_index = jnp.arange(count, dtype=jnp.int32)
    for bit in range(count.bit_length() - 1):
        upper = jnp.bitwise_and(jnp.right_shift(block_index, bit), 1) == 1
        sibling = jnp.maximum(jnp.right_shift(block_index, bit) - 1, 0).astype(jnp.int32)
        picked = block_states[sibling]
        sibling_end = block_ends[sibling]
        gap = jnp.where(upper[:, None], decay_blocks - sibling_end[:, None], -jnp.inf)
        factor = level_blocks[:, :, 1 + bit] * jnp.exp(gap)
        result = result + factor[:, :, None] * jnp.einsum('cik,ckv->civ', query_blocks, picked, precision=highest)
        paired = block_states.reshape(-1, 2, DH, DH)
        paired_ends = block_ends.reshape(-1, 2)
        fade = jnp.exp(paired_ends[:, 1] - paired_ends[:, 0])
        block_states = paired[:, 1] + fade[:, None, None] * paired[:, 0]
        block_ends = paired_ends[:, 1]
    return result.reshape(TOKEN_COUNT, DH)

def reference(tokens, log_decay, w_query, w_key, w_value, w_level, w_out):
    query = jnp.dot(tokens, w_query, preferred_element_type=jnp.float32).astype(jnp.bfloat16).reshape(TOKEN_COUNT, HEAD_GROUP, DH)
    keys = jnp.dot(tokens, w_key, preferred_element_type=jnp.float32).astype(jnp.bfloat16).reshape(TOKEN_COUNT, KV_HEADS, DH)
    values = jnp.dot(tokens, w_value, preferred_element_type=jnp.float32).astype(jnp.bfloat16).reshape(TOKEN_COUNT, KV_HEADS, DH)
    weights = jax.nn.softplus(jnp.dot(tokens, w_level, preferred_element_type=jnp.float32)).reshape(TOKEN_COUNT, HEAD_GROUP, LEVELS)
    decay = jnp.cumsum(log_decay.astype(jnp.float32), axis=0)
    group_size = HEAD_GROUP // KV_HEADS
    keys_heads = jnp.repeat(keys, group_size, axis=1)
    values_heads = jnp.repeat(values, group_size, axis=1)
    outputs = lax.map(head_output, (jnp.transpose(query, (1, 0, 2)), jnp.transpose(keys_heads, (1, 0, 2)), jnp.transpose(values_heads, (1, 0, 2)), jnp.transpose(weights, (1, 0, 2)), decay.T))
    normed = (outputs * lax.rsqrt(lax.optimization_barrier(jnp.mean(outputs * outputs, axis=-1, keepdims=True)) + 1e-05)).astype(jnp.bfloat16)
    per_group = HEAD_GROUP // N_TP
    out_rows = w_out.reshape(HEAD_GROUP, DH, D)
    mixed = jnp.zeros((TOKEN_COUNT, D), jnp.float32)
    for index in range(N_TP):
        lower = index * per_group
        partial_sum = jnp.einsum('htd,hde->te', normed[lower:lower + per_group].astype(jnp.float32), out_rows[lower:lower + per_group].astype(jnp.float32), precision=lax.Precision.HIGHEST)
        rounded = lax.optimization_barrier(partial_sum.astype(jnp.bfloat16))
        mixed = mixed + rounded.astype(jnp.float32)
    return mixed.astype(jnp.bfloat16)
```

```python
import jax
import jax.numpy as jnp
from jax import lax
from jax.sharding import PartitionSpec as P

BLOCK = 128
HIGHEST = lax.Precision.HIGHEST
F32 = jnp.float32
BF16 = jnp.bfloat16


def body(tokens, log_decay, w_query, w_key, w_value, w_level, w_out):
    rows = tokens.shape[0]
    heads = log_decay.shape[1]
    size = w_out.shape[0] // heads
    level_count = w_level.shape[1] // heads
    blocks = rows // BLOCK
    local_bits = blocks.bit_length() - 1
    seq_size = lax.axis_size("seq")
    seq_bits = seq_size.bit_length() - 1
    device = lax.axis_index("seq")

    positions = jnp.arange(rows, dtype=jnp.int32)
    triangle = (positions[:, None] >= positions[None, :]).astype(F32)
    decay = jnp.dot(triangle, log_decay, precision=HIGHEST)
    total = decay[rows - 1]

    def swap(x, bit):
        pairs = [(i, i ^ (1 << bit)) for i in range(seq_size)]
        return lax.ppermute(x, "seq", pairs)

    group, before = total, jnp.zeros_like(total)
    befores, fades = [], []
    for bit in range(seq_bits):
        upper = (jnp.right_shift(device, bit) & 1) == 1
        other = swap(group, bit)
        befores.append(jnp.where(upper, before, -jnp.inf))
        fades.append(jnp.exp(jnp.where(upper, group, other)))
        before = before + jnp.where(upper, other, 0.0)
        group = group + other

    piece = lax.all_gather(tokens, "tp", axis=1, tiled=True)
    dot = lambda a, b: jnp.dot(a, b, preferred_element_type=F32)
    keys = dot(piece, w_key).astype(BF16)
    values = dot(piece, w_value).astype(BF16)
    keep = jnp.exp(total[None, :] - decay)
    weighted = (keep.T[:, :, None] * keys.astype(F32)[None]).astype(BF16)
    state = jnp.einsum("htd,te->hde", weighted, values, preferred_element_type=F32)
    buckets = []
    for bit in range(seq_bits):
        upper = (jnp.right_shift(device, bit) & 1) == 1
        other = swap(state.astype(BF16), bit)
        buckets.append(other)
        wide = other.astype(F32)
        low = jnp.where(upper, wide, state)
        high = jnp.where(upper, state, wide)
        state = high + fades[bit][:, None, None] * low

    query = dot(piece, w_query).astype(BF16).reshape(rows, heads, size)
    level = jax.nn.softplus(dot(piece, w_level)).reshape(rows, heads, level_count)
    qb = query.reshape(blocks, BLOCK, heads, size)
    kb = keys.reshape(blocks, BLOCK, size)
    vb = values.reshape(blocks, BLOCK, size)
    lb = level.reshape(blocks, BLOCK, heads, level_count)
    db = decay.reshape(blocks, BLOCK, heads)
    scores = jnp.einsum("cihd,cjd->hcij", qb, kb, preferred_element_type=F32)
    inside = jnp.arange(BLOCK)
    causal = inside[:, None] >= inside[None, :]
    dh = db.transpose(2, 0, 1)
    gaps = jnp.where(causal, dh[:, :, :, None] - dh[:, :, None, :], -jnp.inf)
    mixing = lb[:, :, :, 0].transpose(2, 0, 1)[:, :, :, None] * jnp.exp(gaps) * scores
    out = jnp.einsum("hcij,cje->hcie", mixing.astype(BF16), vb, preferred_element_type=F32)
    ends = db[:, BLOCK - 1]
    weighted = jnp.exp(ends[:, None] - db).transpose(2, 0, 1)[..., None] * kb.astype(F32)[None]
    small = jnp.einsum("hcjd,cje->hcde", weighted.astype(BF16), vb, preferred_element_type=F32)
    small_ends = ends
    parts = [out[:, c] for c in range(blocks)]
    for bit in range(local_bits):
        for c in range(blocks):
            if (c >> bit) & 1:
                s = (c >> bit) - 1
                factor = lb[c, :, :, 1 + bit] * jnp.exp(db[c] - small_ends[s][None, :])
                got = jnp.einsum("ihd,hde->hie", qb[c], small[:, s].astype(BF16), preferred_element_type=F32)
                parts[c] = parts[c] + factor.T[:, :, None] * got
        fade = jnp.exp(small_ends[1::2] - small_ends[0::2])
        small = small[:, 1::2] + fade.T[:, :, None, None] * small[:, 0::2]
        small_ends = small_ends[1::2]
    combined = jnp.concatenate(parts, axis=1)
    for bit in range(seq_bits):
        factor = level[:, :, 1 + local_bits + bit] * jnp.exp(decay + befores[bit][None, :])
        got = jnp.einsum("thd,hde->hte", query, buckets[bit], preferred_element_type=F32)
        combined = combined + factor.T[:, :, None] * got
    normed = (
        combined * lax.rsqrt(jnp.mean(combined * combined, axis=-1, keepdims=True) + 1e-05)
    ).astype(BF16)
    wide = normed.transpose(1, 0, 2).reshape(rows, heads * size)
    partial = dot(wide, w_out)
    return lax.psum_scatter(partial.astype(BF16), "tp", scatter_dimension=1, tiled=True)


def solution(mesh):
    in_specs = (
        P("seq", "tp"),
        P("seq", "tp"),
        P(None, "tp"),
        P(None, "tp"),
        P(None, "tp"),
        P(None, "tp"),
        P("tp", None),
    )
    return jax.shard_map(
        body, mesh=mesh, in_specs=in_specs, out_specs=P("seq", "tp"), check_vma=False
    )
```

```python
import jax
import jax.numpy as jnp
from jax import lax
from jax.experimental import pallas as pl
from jax.experimental.pallas import tpu as pltpu
from jax.sharding import PartitionSpec as P

BLOCK = 128
F32 = jnp.float32
BF16 = jnp.bfloat16
MESH = pl.DeviceIdType.MESH
NEVER = -1e30
HEADS = 4
SIZE = 128
LEVELS = 9
ROWS = 512
BLOCKS = ROWS // BLOCK
PART = 1024
BITS = 6


def dot(a, b):
    return jnp.dot(a, b, preferred_element_type=F32)


def dot_t(a, b):
    return lax.dot_general(a, b, (((1,), (1,)), ((), ())), preferred_element_type=F32)


def split3(wide):
    high = wide.astype(BF16)
    rest = wide - high.astype(F32)
    middle = rest.astype(BF16)
    low = (rest - middle.astype(F32)).astype(BF16)
    return high, middle, low


def softplus(x):
    return jnp.maximum(x, 0.0) + jnp.log1p(jnp.exp(-jnp.abs(x)))


def kernel(
    x_ref, ld_ref, wq_ref, wk_ref, wv_ref, wl_ref, wo_ref, out_ref,
    xg, wq, wkv, wo, ng,
    ldp, d36, dect, ends, offs, gsend, grecv, coef,
    qb, kb, vb, fac, acc, qs, sb, sb16, run, ssend, bkt,
    tok_s, tok_r, dec_s, dec_r, st_s, st_r, fw_s, fw_r, wo_s, wo_r, nm_s, nm_r, loc,
):
    y = lax.axis_index("tp")
    s = lax.axis_index("seq")
    core = lax.rem(s, 2)
    cx = lax.rem(lax.div(s, 2), 4)
    cz = lax.div(s, 8)
    right, left, across = lax.rem(y + 1, 4), lax.rem(y + 3, 4), lax.rem(y + 2, 4)
    to_right, to_left, to_across = {"tp": right}, {"tp": left}, {"tp": across}
    uppers = [core, lax.rem(cx, 2), lax.div(cx, 2), lax.rem(cz, 2), lax.rem(lax.div(cz, 2), 2), lax.div(cz, 4)]
    mates = [
        s + 1 - 2 * core,
        s + (1 - 2 * uppers[1]) * 2,
        s + (3 - 2 * cx) * 2,
        s + (1 - 2 * uppers[3]) * 8,
        s + (1 - 2 * uppers[4]) * 16,
    ]
    mates = [{"seq": m} for m in mates]
    is_top = cz >= 4
    is_source = jnp.logical_or(cz == 0, cz == 3)
    plane = lax.rem(s, 8)
    near = {"seq": jnp.where(cz == 0, 56, 32) + plane}
    far = {"seq": jnp.where(cz == 0, 48, 40) + plane}
    source = {"seq": jnp.where(cz < 6, 24, 0) + plane}

    def remote(src, dst, send, recv, device):
        return pltpu.make_async_remote_copy(
            src_ref=src, dst_ref=dst, send_sem=send, recv_sem=recv, device_id=device, device_id_type=MESH
        )

    locals_ = [
        pltpu.make_async_copy(x_ref, xg.at[y], loc.at[0]),
        pltpu.make_async_copy(wk_ref, wkv.at[:, pl.ds(0, SIZE)], loc.at[1]),
        pltpu.make_async_copy(wv_ref, wkv.at[:, pl.ds(SIZE, SIZE)], loc.at[2]),
        pltpu.make_async_copy(wq_ref, wq, loc.at[3]),
    ]
    own_out = pltpu.make_async_copy(wo_ref.at[:, pl.ds(pl.multiple_of(y * PART, PART), PART)], wo.at[y], loc.at[5])
    for c in locals_:
        c.start()

    @pl.when(jnp.logical_not(is_top))
    def _():
        bkt[BITS - 1] = jnp.zeros((HEADS * SIZE, SIZE), BF16)

    barrier = pltpu.get_barrier_semaphore()
    for peer in [to_right, to_left, to_across] + mates:
        pl.semaphore_signal(barrier, inc=1, device_id=peer, device_id_type=MESH)

    @pl.when(is_top)
    def _():
        pl.semaphore_signal(barrier, inc=1, device_id=source, device_id_type=MESH)

    pl.semaphore_wait(barrier, 3 + len(mates) + jnp.where(is_source, 2, 0))

    half = BLOCK // 2

    def own_rows(r, side):
        rows = pl.ds(pl.multiple_of(r * BLOCK, BLOCK), BLOCK)
        i = 2 * r + side
        return remote(x_ref.at[rows], xg.at[y, rows], tok_s.at[i], tok_r.at[i], to_left if side else to_right)

    def onward(r, side):
        rows = pl.ds(pl.multiple_of(r * BLOCK + side * half, half), half)
        i = 2 * BLOCKS + 2 * r + side
        owner = right if side else left
        return remote(xg.at[owner, rows], xg.at[owner, rows], tok_s.at[i], tok_r.at[i], to_left if side else to_right)

    for r in range(BLOCKS):
        own_rows(r, 0).start()
        own_rows(r, 1).start()

    def pass_on(r):
        for side in range(2):
            own_rows(r, side).wait_recv()
            onward(r, side).start()

    ldp[...] = jnp.zeros_like(ldp)
    ldp[0:HEADS, :] = ld_ref[...]
    row = lax.broadcasted_iota(jnp.int32, (ROWS, ROWS), 0)
    col = lax.broadcasted_iota(jnp.int32, (ROWS, ROWS), 1)
    lower = (row >= col).astype(F32).astype(BF16)
    upper_tri = (row <= col).astype(F32).astype(BF16)
    wide_row = lax.broadcasted_iota(jnp.int32, (BLOCK, HEADS * LEVELS), 0)
    wide_col = lax.broadcasted_iota(jnp.int32, (BLOCK, HEADS * LEVELS), 1)
    spread = (lax.div(wide_col, LEVELS) == wide_row).astype(F32).astype(BF16)
    level_of = lax.rem(lax.broadcasted_iota(jnp.int32, (8, HEADS * LEVELS), 1), LEVELS)
    spread_decay = sum(dot(lower, dot(p, spread).astype(BF16)) for p in split3(jnp.transpose(ldp[...])))
    d36[...] = spread_decay
    along = sum(dot(p, upper_tri) for p in split3(ldp[0:16, :]))
    dect[...] = along[0:8]
    for c in range(BLOCKS):
        last = (c + 1) * BLOCK - 1
        ends[c] = jnp.broadcast_to(dect[:, last : last + 1], (8, SIZE))
    gsend[0] = jnp.zeros((16, SIZE), F32)
    gsend[0, 0:8] = ends[BLOCKS - 1]
    gsend[0, 8:16, 0 : HEADS * LEVELS] = jnp.broadcast_to(d36[ROWS - 1 : ROWS, :], (8, HEADS * LEVELS))
    before = jnp.zeros((8, HEADS * LEVELS), F32)
    gap_off = jnp.zeros((8, HEADS * LEVELS), F32)
    decay_copies = []
    for bit in range(BITS - 1):
        if bit == 2:
            pass_on(0)
        up = uppers[bit].astype(F32)
        c = remote(gsend.at[bit], grecv.at[bit], dec_s.at[bit], dec_r.at[bit], mates[bit])
        c.start()
        c.wait_recv()
        decay_copies.append(c)
        mine = gsend[bit]
        other = grecv[bit]
        coef[bit, 0] = up + (1.0 - up) * jnp.exp(other[0:8])
        coef[bit, 1] = up * jnp.exp(mine[0:8]) + (1.0 - up)
        gap_off = gap_off + jnp.where(level_of == 3 + bit, up * before + (1.0 - up) * NEVER, 0.0)
        before = before + up * other[8:16, 0 : HEADS * LEVELS]
        if bit < BITS - 2:
            gsend[bit + 1] = mine + other
    up = uppers[BITS - 1].astype(F32)
    gap_off = gap_off + jnp.where(level_of == 3 + BITS - 1, up * before + (1.0 - up) * NEVER, 0.0)
    offs[...] = gap_off
    for c in locals_:
        c.wait()

    def project(r, weights):
        rows = pl.ds(pl.multiple_of(r * BLOCK, BLOCK), BLOCK)
        return sum(dot(xg[i, rows, :], weights[i * PART : (i + 1) * PART, :]) for i in range(4))

    def keys_part(r):
        rows = pl.ds(pl.multiple_of(r * BLOCK, BLOCK), BLOCK)
        both = project(r, wkv)
        values = both[:, SIZE:].astype(BF16)
        kb[rows, :] = both[:, :SIZE].astype(BF16)
        vb[rows, :] = values
        k_t = jnp.transpose(both[:, :SIZE].astype(BF16).astype(F32))
        weight = jnp.exp(ends[r] - dect[:, rows])
        for h in range(HEADS):
            scaled = (k_t * weight[h : h + 1, :]).astype(BF16)
            sb[r, h * SIZE : (h + 1) * SIZE, :] = dot(scaled, values)

    def fade_of(c, before_c, h):
        return jnp.exp(ends[c] - ends[before_c])[h : h + 1, :]

    def query_part(r):
        rows = pl.ds(pl.multiple_of(r * BLOCK, BLOCK), BLOCK)
        qb[rows, :] = project(r, wq).astype(BF16)
        weight = softplus(
            sum(dot_t(xg[i, rows, :], wl_ref[:, i * PART : (i + 1) * PART]) for i in range(4))
        )
        previous = jnp.maximum(r - 1, 0)
        last = d36[pl.ds(previous * BLOCK + BLOCK - 1, 1), :]
        second = d36[2 * BLOCK - 1 : 2 * BLOCK, :]
        odd = lax.rem(r, 2).astype(F32)
        late = lax.div(r, 2).astype(F32)
        kind = level_of[0:1]
        off = jnp.where(kind == 1, odd * -last + (1.0 - odd) * NEVER, offs[0:1, :])
        off = jnp.where(kind == 2, late * -second + (1.0 - late) * NEVER, off)
        here = d36[rows, :]
        power = jnp.where(kind == 0, 0.0, here + off)
        factor = weight * jnp.exp(power)
        fac[rows, :] = factor
        keys = kb[rows, :]
        values = vb[rows, :]
        inside_row = lax.broadcasted_iota(jnp.int32, (BLOCK, BLOCK), 0)
        inside_col = lax.broadcasted_iota(jnp.int32, (BLOCK, BLOCK), 1)
        causal = inside_row >= inside_col
        along_here = dect[:, rows]
        for h in range(HEADS):
            cols = slice(h * SIZE, (h + 1) * SIZE)
            query = qb[rows, cols]
            wide = query.astype(F32)
            scores = dot_t(query, keys)
            gap = here[:, h * LEVELS : h * LEVELS + 1] - along_here[h : h + 1, :]
            mixing = jnp.exp(jnp.where(causal, gap, NEVER)) * scores * factor[:, h * LEVELS : h * LEVELS + 1]
            total = dot(mixing.astype(BF16), values)
            near_query = (wide * factor[:, h * LEVELS + 1 : h * LEVELS + 2]).astype(BF16)
            total = total + dot(near_query, sb[previous, cols, :].astype(BF16))
            late_query = (wide * factor[:, h * LEVELS + 2 : h * LEVELS + 3]).astype(BF16)
            total = total + dot(late_query, sb16[cols, :])
            acc[rows, cols] = total
            for bit in range(BITS):
                at = h * LEVELS + 3 + bit
                qs[bit, rows, cols] = (wide * factor[:, at : at + 1]).astype(BF16)

    def pair_sum():
        for h in range(HEADS):
            cols = slice(h * SIZE, (h + 1) * SIZE)
            sb16[cols, :] = (sb[1, cols, :] + fade_of(1, 0, h) * sb[0, cols, :]).astype(BF16)

    sb16[...] = jnp.zeros_like(sb16)

    for r in range(BLOCKS - 1):
        pass_on(r + 1)
        onward(r, 0).wait_recv()
        onward(r, 1).wait_recv()
        keys_part(r)
        if r == 1:
            pair_sum()
        query_part(jnp.int32(r))
    tail = BLOCKS - 1
    onward(tail, 0).wait_recv()
    onward(tail, 1).wait_recv()
    keys_part(tail)
    for h in range(HEADS):
        cols = slice(h * SIZE, (h + 1) * SIZE)
        first = sb[1, cols, :] + fade_of(1, 0, h) * sb[0, cols, :]
        second = sb[3, cols, :] + fade_of(3, 2, h) * sb[2, cols, :]
        whole = second + fade_of(3, 1, h) * first
        run[cols, :] = whole
        ssend[0, cols, :] = whole.astype(BF16)

    mine = pl.ds(pl.multiple_of(core * 2 * SIZE, 2 * SIZE), 2 * SIZE)
    state_copies = []
    hand_overs = []
    c = remote(ssend.at[0], bkt.at[0], st_s.at[0], st_r.at[0], mates[0])
    c.start()
    state_copies.append(c)

    wide_half = pl.ds(pl.multiple_of(core * 256, 256), 256)
    own_out.start()
    weight_copies = []
    for i, (peer, device) in enumerate(((right, to_right), (left, to_left), (across, to_across))):
        c = remote(
            wo_ref.at[wide_half, pl.ds(pl.multiple_of(peer * PART, PART), PART)],
            wo.at[y, wide_half], wo_s.at[i], wo_r.at[i], device,
        )
        c.start()
        weight_copies.append(c)

    query_part(jnp.int32(tail))

    def take(bit):
        for h in range(HEADS):
            cols = slice(h * SIZE, (h + 1) * SIZE)
            acc[:, cols] += dot(qs[bit, :, cols], bkt[bit, cols, :])

    state_copies[0].wait_recv()
    for bit in range(BITS):
        for i in range(2):
            one = pl.ds(pl.multiple_of((core * 2 + i) * SIZE, SIZE), SIZE)
            if bit < BITS - 1:
                head = pl.ds(core * 2 + i, 1)
                merged = coef[bit, 0, head, :] * run[one, :] + coef[bit, 1, head, :] * bkt[bit, one, :].astype(F32)
                run[one, :] = merged
                ssend[bit + 1, one, :] = merged.astype(BF16)
        nxt = bit + 1
        if nxt < BITS - 1:
            c = remote(ssend.at[nxt, mine], bkt.at[nxt, mine], st_s.at[nxt], st_r.at[nxt], mates[nxt])
            c.start()
            state_copies.append(c)
        elif nxt == BITS - 1:

            @pl.when(is_source)
            def _():
                remote(ssend.at[nxt, mine], bkt.at[nxt, mine], st_s.at[nxt], st_r.at[nxt], near).start()
                remote(ssend.at[nxt, mine], bkt.at[nxt, mine], st_s.at[nxt + 1], st_r.at[nxt], far).start()

        if bit > 0 and bit < BITS - 1:
            hand = remote(bkt.at[bit, mine], bkt.at[bit, mine], fw_s.at[bit], fw_r.at[bit], mates[0])
            hand.start()
            hand_overs.append(hand)
        if bit == 0:
            take(0)
        elif bit > 1:
            hand_overs[bit - 2].wait_recv()
            take(bit - 1)
        if nxt < BITS - 1:
            state_copies[nxt].wait_recv()
        elif nxt == BITS - 1:
            final = remote(bkt.at[nxt, mine], bkt.at[nxt, mine], fw_s.at[nxt], fw_r.at[nxt], mates[0])

            @pl.when(is_top)
            def _():
                remote(ssend.at[nxt, mine], bkt.at[nxt, mine], st_s.at[nxt], st_r.at[nxt], source).wait_recv()
                final.start()

            @pl.when(is_top)
            def _():
                final.wait_recv()

    def own_normed(r, side):
        rows = pl.ds(r * BLOCK, BLOCK)
        i = 2 * r + side
        return remote(ng.at[y, rows], ng.at[y, rows], nm_s.at[i], nm_r.at[i], to_left if side else to_right)

    def onward_normed(r, side):
        rows = pl.ds(r * BLOCK + side * half, half)
        i = 2 * BLOCKS + 2 * r + side
        owner = right if side else left
        return remote(ng.at[owner, rows], ng.at[owner, rows], nm_s.at[i], nm_r.at[i], to_left if side else to_right)

    for r in range(BLOCKS):
        rows = slice(r * BLOCK, (r + 1) * BLOCK)
        for h in range(HEADS):
            cols = slice(h * SIZE, (h + 1) * SIZE)
            value = acc[rows, cols] + dot(qs[BITS - 1, rows, cols], bkt[BITS - 1, cols, :])
            mean = jnp.mean(value * value, axis=-1, keepdims=True)
            ng[y, rows, cols] = (value * lax.rsqrt(mean + 1e-05)).astype(BF16)
        own_normed(r, 0).start()
        own_normed(r, 1).start()

    share = []
    for i, owner in enumerate((left, right, across)):
        weight_copies[i].wait_recv()
        c = remote(wo.at[owner, wide_half], wo.at[owner, wide_half], wo_s.at[3 + i], wo_r.at[3 + i], mates[0])
        c.start()
        share.append(c)
    own_out.wait()

    def pass_normed(r):
        for side in range(2):
            own_normed(r, side).wait_recv()
            onward_normed(r, side).start()

    pass_normed(0)
    for c in share:
        c.wait_recv()
    for r in range(BLOCKS):
        if r + 1 < BLOCKS:
            pass_normed(r + 1)
        onward_normed(r, 0).wait_recv()
        onward_normed(r, 1).wait_recv()
        rows = slice(r * BLOCK, (r + 1) * BLOCK)
        out_ref[rows, :] = sum(dot(ng[i, rows, :], wo[i]) for i in range(4)).astype(BF16)

    for r in range(BLOCKS):
        for side in range(2):
            own_rows(r, side).wait_send()
            onward(r, side).wait_send()
            own_normed(r, side).wait_send()
            onward_normed(r, side).wait_send()
    for c in decay_copies + state_copies + hand_overs + weight_copies + share:
        c.wait_send()

    @pl.when(is_source)
    def _():
        last_bit = BITS - 1
        remote(ssend.at[last_bit, mine], bkt.at[last_bit, mine], st_s.at[last_bit], st_r.at[last_bit], near).wait_send()
        remote(ssend.at[last_bit, mine], bkt.at[last_bit, mine], st_s.at[last_bit + 1], st_r.at[last_bit], far).wait_send()

    @pl.when(is_top)
    def _():
        final.wait_send()


def body(tokens, log_decay, w_query, w_key, w_value, w_level, w_out):
    hbm = pl.BlockSpec(memory_space=pl.ANY)
    vmem = pl.BlockSpec(memory_space=pltpu.VMEM)
    dma = pltpu.SemaphoreType.DMA
    wide = HEADS * LEVELS
    return pl.pallas_call(
        kernel,
        name="layer",
        out_shape=pltpu.VMEM((ROWS, PART), BF16),
        in_specs=[hbm, vmem, hbm, hbm, hbm, vmem, hbm],
        out_specs=vmem,
        scratch_shapes=[
            pltpu.VMEM((4, ROWS, PART), BF16),
            pltpu.VMEM((4 * PART, HEADS * SIZE), BF16),
            pltpu.VMEM((4 * PART, 2 * SIZE), BF16),
            pltpu.VMEM((4, HEADS * SIZE, PART), BF16),
            pltpu.VMEM((4, ROWS, HEADS * SIZE), BF16),
            pltpu.VMEM((SIZE, ROWS), F32),
            pltpu.VMEM((ROWS, wide), F32),
            pltpu.VMEM((8, ROWS), F32),
            pltpu.VMEM((BLOCKS, 8, SIZE), F32),
            pltpu.VMEM((8, wide), F32),
            pltpu.VMEM((BITS - 1, 16, SIZE), F32),
            pltpu.VMEM((BITS - 1, 16, SIZE), F32),
            pltpu.VMEM((BITS - 1, 2, 8, SIZE), F32),
            pltpu.VMEM((ROWS, HEADS * SIZE), BF16),
            pltpu.VMEM((ROWS, SIZE), BF16),
            pltpu.VMEM((ROWS, SIZE), BF16),
            pltpu.VMEM((ROWS, wide), F32),
            pltpu.VMEM((ROWS, HEADS * SIZE), F32),
            pltpu.VMEM((BITS, ROWS, HEADS * SIZE), BF16),
            pltpu.VMEM((BLOCKS, HEADS * SIZE, SIZE), F32),
            pltpu.VMEM((HEADS * SIZE, SIZE), BF16),
            pltpu.VMEM((HEADS * SIZE, SIZE), F32),
            pltpu.VMEM((BITS, HEADS * SIZE, SIZE), BF16),
            pltpu.VMEM((BITS, HEADS * SIZE, SIZE), BF16),
            dma((4 * BLOCKS,)), dma((4 * BLOCKS,)),
            dma((BITS - 1,)), dma((BITS - 1,)),
            dma((BITS + 1,)), dma((BITS + 1,)),
            dma((BITS,)), dma((BITS,)),
            dma((6,)), dma((6,)),
            dma((4 * BLOCKS,)), dma((4 * BLOCKS,)),
            dma((6,)),
        ],
        compiler_params=pltpu.CompilerParams(
            collective_id=0, has_side_effects=True, vmem_limit_bytes=56 << 20
        ),
        cost_estimate=pl.CostEstimate(flops=7_000_000_000, bytes_accessed=14_000_000, transcendentals=400_000),
    )(tokens, log_decay.T, w_query, w_key, w_value, w_level.T, w_out)


def solution(mesh):
    in_specs = (
        P("seq", "tp"),
        P("seq", "tp"),
        P(None, "tp"),
        P(None, "tp"),
        P(None, "tp"),
        P(None, "tp"),
        P("tp", None),
    )
    return jax.shard_map(
        body, mesh=mesh, in_specs=in_specs, out_specs=P("seq", "tp"), check_vma=False
    )
```

```python
import jax
import jax.numpy as jnp
from jax import lax
from jax.experimental import pallas as pl
from jax.experimental.pallas import tpu as pltpu
from jax.sharding import PartitionSpec as P

BLOCK = 128
F32 = jnp.float32
BF16 = jnp.bfloat16
MESH = pl.DeviceIdType.MESH
NEVER = -1e30
HEADS = 4
SIZE = 128
LEVELS = 9
ROWS = 512
BLOCKS = ROWS // BLOCK
PART = 1024
BITS = 6


def dot(a, b):
    return jnp.dot(a, b, preferred_element_type=F32)


def dot_t(a, b):
    return lax.dot_general(a, b, (((1,), (1,)), ((), ())), preferred_element_type=F32)


def split3(wide):
    high = wide.astype(BF16)
    rest = wide - high.astype(F32)
    middle = rest.astype(BF16)
    low = (rest - middle.astype(F32)).astype(BF16)
    return high, middle, low


def softplus(x):
    return jnp.maximum(x, 0.0) + jnp.log1p(jnp.exp(-jnp.abs(x)))


def kernel(
    x_ref, ld_ref, wq_ref, wk_ref, wv_ref, wl_ref, wo_ref, out_ref,
    xg, wq, wkv, wown, wop, ng, pacc,
    ldp, d36, dect, ends, offs, gsend, grecv, coef, pair, xin,
    qb, kb, vb, acc, qs, sb, sb16, run, ssend, bkt,
    tok_s, tok_r, dec_s, dec_r, st_s, st_r, xs, xr, fw_s, fw_r, wo_s, wo_r, nm_s, nm_r, loc,
):
    y = lax.axis_index("tp")
    s = lax.axis_index("seq")
    core = lax.rem(s, 2)
    cx = lax.rem(lax.div(s, 2), 4)
    cz = lax.div(s, 8)
    right, left, across = lax.rem(y + 1, 4), lax.rem(y + 3, 4), lax.rem(y + 2, 4)
    to_right, to_left, to_across = {"tp": right}, {"tp": left}, {"tp": across}
    uppers = [core, lax.rem(cx, 2), lax.div(cx, 2), lax.rem(cz, 2), lax.rem(lax.div(cz, 2), 2), lax.div(cz, 4)]
    mates = [
        s + 1 - 2 * core,
        s + (1 - 2 * uppers[1]) * 2,
        s + (3 - 2 * cx) * 2,
        s + (1 - 2 * uppers[3]) * 8,
        s + (1 - 2 * uppers[4]) * 16,
    ]
    opposite = {"seq": s + (1 - 2 * uppers[5]) * 32}
    x_across = {"seq": s + (1 - 2 * uppers[2]) * 4}
    mates = [{"seq": m} for m in mates]
    is_top = cz >= 4
    is_source = jnp.logical_or(cz == 0, cz == 3)
    plane = lax.rem(s, 8)
    near = {"seq": jnp.where(cz == 0, 56, 32) + plane}
    far = {"seq": jnp.where(cz == 0, 48, 40) + plane}
    source = {"seq": jnp.where(cz < 6, 24, 0) + plane}

    def remote(src, dst, send, recv, device):
        return pltpu.make_async_remote_copy(
            src_ref=src, dst_ref=dst, send_sem=send, recv_sem=recv, device_id=device, device_id_type=MESH
        )

    locals_ = [
        pltpu.make_async_copy(x_ref, xg.at[y], loc.at[0]),
        pltpu.make_async_copy(wk_ref, wkv.at[:, pl.ds(0, SIZE)], loc.at[1]),
        pltpu.make_async_copy(wv_ref, wkv.at[:, pl.ds(SIZE, SIZE)], loc.at[2]),
        pltpu.make_async_copy(wq_ref, wq, loc.at[3]),
    ]
    own_out = pltpu.make_async_copy(wo_ref.at[:, pl.ds(pl.multiple_of(y * PART, PART), PART)], wown, loc.at[4])
    for c in locals_:
        c.start()

    @pl.when(jnp.logical_not(is_top))
    def _():
        bkt[BITS - 1] = jnp.zeros((HEADS * SIZE, SIZE), BF16)

    barrier = pltpu.get_barrier_semaphore()
    for peer in [to_right, to_left, to_across, opposite, x_across] + mates:
        pl.semaphore_signal(barrier, inc=1, device_id=peer, device_id_type=MESH)

    @pl.when(is_top)
    def _():
        pl.semaphore_signal(barrier, inc=1, device_id=source, device_id_type=MESH)

    pl.semaphore_wait(barrier, 5 + len(mates) + jnp.where(is_source, 2, 0))

    half = BLOCK // 2

    def own_rows(r, side):
        rows = pl.ds(pl.multiple_of(r * BLOCK, BLOCK), BLOCK)
        i = 2 * r + side
        return remote(x_ref.at[rows], xg.at[y, rows], tok_s.at[i], tok_r.at[i], to_left if side else to_right)

    def onward(r, side):
        rows = pl.ds(pl.multiple_of(r * BLOCK + side * half, half), half)
        i = 2 * BLOCKS + 2 * r + side
        owner = right if side else left
        return remote(xg.at[owner, rows], xg.at[owner, rows], tok_s.at[i], tok_r.at[i], to_left if side else to_right)

    wide_cols = pl.ds(pl.multiple_of(core * 512, 512), 512)
    cols_a = pl.ds(pl.multiple_of(core * 512, 256), 256)
    cols_b = pl.ds(pl.multiple_of(core * 512 + 256, 256), 256)
    piece = cx * 8 + cz

    def some_rows(start, count):
        return pl.ds(pl.multiple_of(start * 16, 16), count * 16)

    def spread_copy(i, rows, cols, device):
        part = wop.at[:, rows, cols]
        return remote(part, part, wo_s.at[i], wo_r.at[i], device)

    fetch = []
    for i, (peer, device) in enumerate(((right, to_right), (left, to_left), (across, to_across))):
        there = pl.ds(pl.multiple_of(peer * PART + core * 512, 512), 512)
        rows = some_rows(piece, 1)
        fetch.append(remote(wo_ref.at[rows, there], wop.at[i, rows, wide_cols], wo_s.at[i], wo_r.at[i], device))
    over_z = [
        spread_copy(3, some_rows(piece, 1), wide_cols, mates[3]),
        spread_copy(4, some_rows(piece - lax.rem(cz, 2), 2), wide_cols, mates[4]),
        spread_copy(5, some_rows(piece - lax.rem(cz, 4), 4), wide_cols, opposite),
    ]
    over_x = [
        spread_copy(6, some_rows(cx * 8, 8), cols_a, mates[1]),
        spread_copy(7, some_rows(cx * 8, 8), cols_b, mates[2]),
    ]
    over_x2 = [
        spread_copy(8, some_rows(lax.div(cx, 2) * 16, 16), cols_a, mates[2]),
        spread_copy(9, some_rows(cx * 8, 8), cols_b, mates[1]),
        spread_copy(10, some_rows((3 - cx) * 8, 8), cols_b, mates[1]),
    ]
    share = spread_copy(11, pl.ds(0, ROWS), wide_cols, mates[0])
    for c in fetch:
        c.start()

    half = BLOCK // 2

    def own_rows(r, side):
        rows = pl.ds(r * BLOCK, BLOCK)
        i = 2 * r + side
        return remote(x_ref.at[rows], xg.at[y, rows], tok_s.at[i], tok_r.at[i], to_left if side else to_right)

    def onward(r, side):
        rows = pl.ds(r * BLOCK + side * half, half)
        i = 2 * BLOCKS + 2 * r + side
        owner = right if side else left
        return remote(xg.at[owner, rows], xg.at[owner, rows], tok_s.at[i], tok_r.at[i], to_left if side else to_right)

    for r in range(3):
        own_rows(r, 0).start()
        own_rows(r, 1).start()

    def pass_on(r):
        for side in range(2):
            own_rows(r, side).wait_recv()
            onward(r, side).start()
            if r + 3 < BLOCKS:
                own_rows(r + 3, side).start()

    ldp[...] = jnp.zeros_like(ldp)
    ldp[0:HEADS, :] = ld_ref[...]
    row = lax.broadcasted_iota(jnp.int32, (ROWS, ROWS), 0)
    col = lax.broadcasted_iota(jnp.int32, (ROWS, ROWS), 1)
    lower = (row >= col).astype(F32).astype(BF16)
    upper_tri = (row <= col).astype(F32).astype(BF16)
    wide_row = lax.broadcasted_iota(jnp.int32, (BLOCK, HEADS * LEVELS), 0)
    wide_col = lax.broadcasted_iota(jnp.int32, (BLOCK, HEADS * LEVELS), 1)
    spread = (lax.div(wide_col, LEVELS) == wide_row).astype(F32).astype(BF16)
    level_of = lax.rem(lax.broadcasted_iota(jnp.int32, (8, HEADS * LEVELS), 1), LEVELS)
    spread_decay = sum(dot(lower, dot(p, spread).astype(BF16)) for p in split3(jnp.transpose(ldp[...])))
    d36[...] = spread_decay
    along = sum(dot(p, upper_tri) for p in split3(ldp[0:16, :]))
    dect[...] = along[0:8]
    for c in range(BLOCKS):
        last = (c + 1) * BLOCK - 1
        ends[c] = jnp.broadcast_to(dect[:, last : last + 1], (8, SIZE))
    gsend[0] = jnp.zeros((24, SIZE), F32)
    gsend[0, 0:8] = ends[BLOCKS - 1]
    gsend[0, 8:16, 0 : HEADS * LEVELS] = jnp.broadcast_to(d36[ROWS - 1 : ROWS, :], (8, HEADS * LEVELS))
    before = jnp.zeros((8, HEADS * LEVELS), F32)
    gap_off = jnp.zeros((8, HEADS * LEVELS), F32)
    decay_copies = []
    for bit in range(BITS - 1):
        if bit == 2:
            for c in fetch:
                c.wait_recv()
            over_z[0].start()
        if bit == 3:
            over_z[0].wait_recv()
            over_z[1].start()
            pass_on(0)
        if bit == 4:
            over_z[1].wait_recv()
            over_z[2].start()
            pass_on(1)
        up = uppers[bit].astype(F32)
        c = remote(gsend.at[bit], grecv.at[bit], dec_s.at[bit], dec_r.at[bit], mates[bit])
        c.start()
        c.wait_recv()
        decay_copies.append(c)
        mine = gsend[bit]
        other = grecv[bit]
        coef[bit, 0] = up + (1.0 - up) * jnp.exp(other[0:8])
        coef[bit, 1] = up * jnp.exp(mine[0:8]) + (1.0 - up)
        gap_off = gap_off + jnp.where(level_of == 3 + bit, up * before + (1.0 - up) * NEVER, 0.0)
        before = before + up * other[8:16, 0 : HEADS * LEVELS]
        if bit < BITS - 2:
            gsend[bit + 1, 0:16] = mine[0:16] + other[0:16]
            gsend[bit + 1, 16:24] = mine[0:8]
        if bit == 2:
            third = other[16:24]
            fourth = other[0:8] - third
            side = uppers[1].astype(F32)
            pair[0] = side * jnp.exp(fourth) + (1.0 - side)
            pair[1] = side + (1.0 - side) * jnp.exp(third)
    up = uppers[BITS - 1].astype(F32)
    gap_off = gap_off + jnp.where(level_of == 3 + BITS - 1, up * before + (1.0 - up) * NEVER, 0.0)
    offs[...] = gap_off
    for c in locals_:
        c.wait()

    owners = (y, left, right, across)

    def project(r, weights, who=owners):
        rows = pl.ds(r * BLOCK, BLOCK)
        return sum(dot(xg[i, rows, :], weights[pl.ds(pl.multiple_of(i * PART, PART), PART), :]) for i in who)

    def keys_part(r):
        rows = pl.ds(r * BLOCK, BLOCK)
        part = project(r, wkv, owners[:3])
        onward(r, 0).wait_recv()
        onward(r, 1).wait_recv()
        both = part + project(r, wkv, owners[3:])
        values = both[:, SIZE:].astype(BF16)
        kb[rows, :] = both[:, :SIZE].astype(BF16)
        vb[rows, :] = values
        k_t = jnp.transpose(both[:, :SIZE].astype(BF16).astype(F32))
        weight = jnp.exp(ends[r] - dect[:, r * BLOCK : (r + 1) * BLOCK])
        for h in range(HEADS):
            scaled = (k_t * weight[h : h + 1, :]).astype(BF16)
            sb[r, h * SIZE : (h + 1) * SIZE, :] = dot(scaled, values)

    def fade_of(c, before_c, h):
        return jnp.exp(ends[c] - ends[before_c])[h : h + 1, :]

    def query_part(r):
        rows = slice(r * BLOCK, (r + 1) * BLOCK)
        qb[rows, :] = project(r, wq).astype(BF16)
        weight = softplus(sum(dot_t(xg[i, rows, :], wl_ref[:, i * PART : (i + 1) * PART]) for i in range(4)))
        kind = level_of[0:1]
        off = offs[0:1, :]
        off = jnp.where(kind == 1, -d36[r * BLOCK - 1 : r * BLOCK, :] if r % 2 else NEVER, off)
        off = jnp.where(kind == 2, -d36[2 * BLOCK - 1 : 2 * BLOCK, :] if r >= 2 else NEVER, off)
        here = d36[rows, :]
        power = jnp.where(kind == 0, 0.0, here + off)
        factor = weight * jnp.exp(power)
        keys = kb[rows, :]
        values = vb[rows, :]
        inside_row = lax.broadcasted_iota(jnp.int32, (BLOCK, BLOCK), 0)
        inside_col = lax.broadcasted_iota(jnp.int32, (BLOCK, BLOCK), 1)
        causal = inside_row >= inside_col
        along_here = dect[:, rows]
        for h in range(HEADS):
            cols = slice(h * SIZE, (h + 1) * SIZE)
            query = qb[rows, cols]
            wide = query.astype(F32)
            scores = dot_t(query, keys)
            gap = here[:, h * LEVELS : h * LEVELS + 1] - along_here[h : h + 1, :]
            mixing = jnp.exp(jnp.where(causal, gap, NEVER)) * scores * factor[:, h * LEVELS : h * LEVELS + 1]
            total = dot(mixing.astype(BF16), values)
            if r % 2:
                near_query = (wide * factor[:, h * LEVELS + 1 : h * LEVELS + 2]).astype(BF16)
                total = total + dot(near_query, sb[r - 1, cols, :].astype(BF16))
            if r >= 2:
                late_query = (wide * factor[:, h * LEVELS + 2 : h * LEVELS + 3]).astype(BF16)
                total = total + dot(late_query, sb16[cols, :])
            acc[rows, cols] = total
            for bit in range(BITS):
                at = h * LEVELS + 3 + bit
                qs[bit, rows, cols] = (wide * factor[:, at : at + 1]).astype(BF16)

    def pair_sum():
        for h in range(HEADS):
            cols = slice(h * SIZE, (h + 1) * SIZE)
            sb16[cols, :] = (sb[1, cols, :] + fade_of(1, 0, h) * sb[0, cols, :]).astype(BF16)

    pass_on(2)
    keys_part(0)
    over_z[2].wait_recv()
    for c in over_x:
        c.start()
    query_part(0)
    pass_on(3)
    keys_part(1)
    pair_sum()
    query_part(1)
    keys_part(2)
    keys_part(BLOCKS - 1)
    for h in range(HEADS):
        cols = slice(h * SIZE, (h + 1) * SIZE)
        first = sb[1, cols, :] + fade_of(1, 0, h) * sb[0, cols, :]
        second = sb[3, cols, :] + fade_of(3, 2, h) * sb[2, cols, :]
        whole = second + fade_of(3, 1, h) * first
        run[cols, :] = whole
        ssend[0, cols, :] = whole.astype(BF16)

    last_bit = BITS - 1

    def head_rows(wave):
        return pl.ds(pl.multiple_of((2 * wave + core) * SIZE, SIZE), SIZE)

    def state_copy(bit, wave):
        rows = pl.ds(2 * wave * SIZE, 2 * SIZE) if bit == 0 else head_rows(wave)
        i = 2 * bit + wave
        return remote(ssend.at[bit, rows], bkt.at[bit, rows], st_s.at[i], st_r.at[i], mates[bit])

    def top_copy(wave, device, place):
        rows = head_rows(wave)
        i = 2 * last_bit + wave
        return remote(ssend.at[last_bit, rows], bkt.at[last_bit, rows], st_s.at[i + 2 * place], st_r.at[i], device)

    def hand_over(bit, wave):
        rows = head_rows(wave)
        i = 2 * bit + wave
        return remote(bkt.at[bit, rows], bkt.at[bit, rows], fw_s.at[i], fw_r.at[i], mates[0])

    for wave in range(2):
        state_copy(0, wave).start()
    own_out.start()

    def take(bit):
        for h in range(HEADS):
            cols = slice(h * SIZE, (h + 1) * SIZE)
            acc[:, cols] += dot(qs[bit, :, cols], bkt[bit, cols, :])

    def corner(wave, third):
        rows = head_rows(wave)
        if third:
            return remote(ssend.at[1, rows], xin.at[0, rows], st_s.at[4 + wave], st_r.at[4 + wave], mates[2])
        return remote(ssend.at[1, rows], xin.at[1, rows], xs.at[wave], xr.at[wave], x_across)

    def scale(row, wave):
        return row[pl.ds(2 * wave + core, 1), :]

    def merge(bit, wave, other):
        one = head_rows(wave)
        return scale(coef.at[bit, 0], wave) * run[one, :] + scale(coef.at[bit, 1], wave) * other

    for wave in range(2):
        one = head_rows(wave)
        state_copy(0, wave).wait_recv()
        merged = merge(0, wave, bkt[0, one, :].astype(F32))
        run[one, :] = merged
        ssend[1, one, :] = merged.astype(BF16)
        corner(wave, False).start()
        state_copy(1, wave).start()
        corner(wave, True).start()
    query_part(2)
    for wave in range(2):
        one = head_rows(wave)
        state_copy(1, wave).wait_recv()
        corner(wave, True).wait_recv()
        corner(wave, False).wait_recv()
        run[one, :] = merge(1, wave, bkt[1, one, :].astype(F32))
        second = scale(pair.at[0], wave) * xin[0, one, :].astype(F32) + scale(pair.at[1], wave) * xin[1, one, :].astype(F32)
        merged = merge(2, wave, second)
        run[one, :] = merged
        ssend[3, one, :] = merged.astype(BF16)
        state_copy(3, wave).start()
        bkt[2, one, :] = second.astype(BF16)
        hand_over(1, wave).start()
        hand_over(2, wave).start()
    for c in over_x:
        c.wait_recv()
    for c in over_x2:
        c.start()
    query_part(BLOCKS - 1)
    for wave in range(2):
        one = head_rows(wave)
        state_copy(3, wave).wait_recv()
        merged = merge(3, wave, bkt[3, one, :].astype(F32))
        run[one, :] = merged
        ssend[4, one, :] = merged.astype(BF16)
        state_copy(4, wave).start()
        hand_over(3, wave).start()
    take(0)
    for wave in range(2):
        hand_over(1, wave).wait_recv()
    take(1)
    for wave in range(2):
        one = head_rows(wave)
        state_copy(4, wave).wait_recv()
        ssend[last_bit, one, :] = merge(4, wave, bkt[4, one, :].astype(F32)).astype(BF16)

        @pl.when(is_source)
        def _(wave=wave):
            top_copy(wave, near, 0).start()
            top_copy(wave, far, 1).start()

        hand_over(4, wave).start()
    for bit in (2, 3):
        for wave in range(2):
            hand_over(bit, wave).wait_recv()
        take(bit)

    many = ROWS // 2

    def own_normed(u, side):
        part = ng.at[y, u // 2, pl.ds(u % 2 * many, many)]
        i = 2 * u + side
        return remote(part, part, nm_s.at[i], nm_r.at[i], to_left if side else to_right)

    def onward_normed(u, side):
        part = ng.at[right if side else left, u // 2, pl.ds(u % 2 * many + side * BLOCK, BLOCK)]
        i = 8 + 2 * u + side
        return remote(part, part, nm_s.at[i], nm_r.at[i], to_left if side else to_right)

    for wave in range(2):

        @pl.when(is_top)
        def _(wave=wave):
            top_copy(wave, source, 0).wait_recv()
            hand_over(last_bit, wave).start()

    for wave in range(2):
        hand_over(last_bit - 1, wave).wait_recv()
    take(last_bit - 1)
    for wave in range(2):

        @pl.when(is_top)
        def _(wave=wave):
            hand_over(last_bit, wave).wait_recv()

        for part in range(2):
            rows = slice(part * many, (part + 1) * many)
            for i in range(2):
                h = 2 * wave + i
                cols = slice(h * SIZE, (h + 1) * SIZE)
                value = acc[rows, cols] + dot(qs[last_bit, rows, cols], bkt[last_bit, cols, :])
                mean = jnp.mean(value * value, axis=-1, keepdims=True)
                ng[y, wave, rows, i * SIZE : (i + 1) * SIZE] = (value * lax.rsqrt(mean + 1e-05)).astype(BF16)
            own_normed(2 * wave + part, 0).start()
            own_normed(2 * wave + part, 1).start()

    def pass_normed(u):
        for side in range(2):
            own_normed(u, side).wait_recv()
            onward_normed(u, side).start()

    for c in over_x2:
        c.wait_recv()
    share.start()
    pass_normed(0)
    own_out.wait()
    share.wait_recv()

    def place(u):
        wave = u // 2
        return wave, slice(u % 2 * many, (u % 2 + 1) * many), slice(wave * 256, (wave + 1) * 256)

    for u in range(4):
        if u > 0:
            pass_normed(u)
        wave, rows, depth = place(u)
        product = dot(ng[y, wave, rows, :], wown[depth, :])
        product = product + dot(ng[left, wave, rows, :], wop[0, depth, :])
        product = product + dot(ng[right, wave, rows, :], wop[1, depth, :])
        pacc[wave, rows, :] = product
    for u in range(4):
        onward_normed(u, 0).wait_recv()
        onward_normed(u, 1).wait_recv()
        wave, rows, depth = place(u)
        product = pacc[wave, rows, :] + dot(ng[across, wave, rows, :], wop[2, depth, :])
        if wave == 0:
            pacc[0, rows, :] = product
        else:
            out_ref[rows, :] = (pacc[0, rows, :] + product).astype(BF16)

    for r in range(BLOCKS):
        for side in range(2):
            own_rows(r, side).wait_send()
            onward(r, side).wait_send()
            own_normed(r, side).wait_send()
            onward_normed(r, side).wait_send()
    for c in decay_copies + fetch + over_z + over_x + over_x2 + [share]:
        c.wait_send()
    for wave in range(2):
        corner(wave, True).wait_send()
        corner(wave, False).wait_send()
        for bit in range(last_bit):
            if bit != 2:
                state_copy(bit, wave).wait_send()
            if bit > 0:
                hand_over(bit, wave).wait_send()

        @pl.when(is_source)
        def _(wave=wave):
            top_copy(wave, near, 0).wait_send()
            top_copy(wave, far, 1).wait_send()

        @pl.when(is_top)
        def _(wave=wave):
            hand_over(last_bit, wave).wait_send()


def body(tokens, log_decay, w_query, w_key, w_value, w_level, w_out):
    hbm = pl.BlockSpec(memory_space=pl.ANY)
    vmem = pl.BlockSpec(memory_space=pltpu.VMEM)
    dma = pltpu.SemaphoreType.DMA
    wide = HEADS * LEVELS
    return pl.pallas_call(
        kernel,
        name="layer",
        out_shape=pltpu.VMEM((ROWS, PART), BF16),
        in_specs=[hbm, vmem, hbm, hbm, hbm, vmem, hbm],
        out_specs=vmem,
        scratch_shapes=[
            pltpu.VMEM((4, ROWS, PART), BF16),
            pltpu.VMEM((4 * PART, HEADS * SIZE), BF16),
            pltpu.VMEM((4 * PART, 2 * SIZE), BF16),
            pltpu.VMEM((HEADS * SIZE, PART), BF16),
            pltpu.VMEM((3, HEADS * SIZE, PART), BF16),
            pltpu.VMEM((4, 2, ROWS, 2 * SIZE), BF16),
            pltpu.VMEM((2, ROWS, PART), F32),
            pltpu.VMEM((SIZE, ROWS), F32),
            pltpu.VMEM((ROWS, wide), F32),
            pltpu.VMEM((8, ROWS), F32),
            pltpu.VMEM((BLOCKS, 8, SIZE), F32),
            pltpu.VMEM((8, wide), F32),
            pltpu.VMEM((BITS - 1, 24, SIZE), F32),
            pltpu.VMEM((BITS - 1, 24, SIZE), F32),
            pltpu.VMEM((BITS - 1, 2, 8, SIZE), F32),
            pltpu.VMEM((2, 8, SIZE), F32),
            pltpu.VMEM((2, HEADS * SIZE, SIZE), BF16),
            pltpu.VMEM((ROWS, HEADS * SIZE), BF16),
            pltpu.VMEM((ROWS, SIZE), BF16),
            pltpu.VMEM((ROWS, SIZE), BF16),
            pltpu.VMEM((ROWS, HEADS * SIZE), F32),
            pltpu.VMEM((BITS, ROWS, HEADS * SIZE), BF16),
            pltpu.VMEM((BLOCKS, HEADS * SIZE, SIZE), F32),
            pltpu.VMEM((HEADS * SIZE, SIZE), BF16),
            pltpu.VMEM((HEADS * SIZE, SIZE), F32),
            pltpu.VMEM((BITS, HEADS * SIZE, SIZE), BF16),
            pltpu.VMEM((BITS, HEADS * SIZE, SIZE), BF16),
            dma((4 * BLOCKS,)), dma((4 * BLOCKS,)),
            dma((BITS - 1,)), dma((BITS - 1,)),
            dma((2 * BITS + 2,)), dma((2 * BITS,)),
            dma((2,)), dma((2,)),
            dma((2 * BITS,)), dma((2 * BITS,)),
            dma((12,)), dma((12,)),
            dma((4 * BLOCKS,)), dma((4 * BLOCKS,)),
            dma((5,)),
        ],
        compiler_params=pltpu.CompilerParams(
            collective_id=0, has_side_effects=True, vmem_limit_bytes=56 << 20
        ),
        cost_estimate=pl.CostEstimate(flops=7_000_000_000, bytes_accessed=14_000_000, transcendentals=400_000),
    )(tokens, log_decay.T, w_query, w_key, w_value, w_level.T, w_out)


def solution(mesh):
    in_specs = (
        P("seq", "tp"),
        P("seq", "tp"),
        P(None, "tp"),
        P(None, "tp"),
        P(None, "tp"),
        P(None, "tp"),
        P("tp", None),
    )
    return jax.shard_map(
        body, mesh=mesh, in_specs=in_specs, out_specs=P("seq", "tp"), check_vma=False
    )
```

```python
import jax
import jax.numpy as jnp
from jax import lax
from jax.experimental import pallas as pl
from jax.experimental.pallas import tpu as pltpu
from jax.sharding import PartitionSpec as P

BLOCK = 128
F32 = jnp.float32
BF16 = jnp.bfloat16
MESH = pl.DeviceIdType.MESH
NEVER = -1e30
HEADS = 4
SIZE = 128
LEVELS = 9
ROWS = 512
BLOCKS = ROWS // BLOCK
PART = 1024
BITS = 6
EARLY = 2
LATE = ROWS - EARLY * BLOCK


def dot(a, b):
    return jnp.dot(a, b, preferred_element_type=F32)


def dot_t(a, b):
    return lax.dot_general(a, b, (((1,), (1,)), ((), ())), preferred_element_type=F32)


def split3(wide):
    high = wide.astype(BF16)
    rest = wide - high.astype(F32)
    middle = rest.astype(BF16)
    low = (rest - middle.astype(F32)).astype(BF16)
    return high, middle, low


def softplus(x):
    return jnp.maximum(x, 0.0) + jnp.log1p(jnp.exp(-jnp.abs(x)))


def kernel(
    x_ref, ld_ref, wq_ref, wk_ref, wv_ref, wl_ref, wo_ref, out_ref,
    xg, wq, wkv, wkp, psend, prec, wown, wop, ng, pacc,
    ldp, d36, dect, ends, offs, gsend, grecv, coef, pair, xin,
    qb, kb, vb, acc, qs, sb, sb16, run, ssend, bkt,
    tok_s, tok_r, dec_s, dec_r, st_s, st_r, xs, xr, fw_s, fw_r, wo_s, wo_r, kv_s, kv_r, nm_s, nm_r, loc,
):
    y = lax.axis_index("tp")
    s = lax.axis_index("seq")
    core = lax.rem(s, 2)
    cx = lax.rem(lax.div(s, 2), 4)
    cz = lax.div(s, 8)
    right, left, across = lax.rem(y + 1, 4), lax.rem(y + 3, 4), lax.rem(y + 2, 4)
    to_right, to_left, to_across = {"tp": right}, {"tp": left}, {"tp": across}
    uppers = [core, lax.rem(cx, 2), lax.div(cx, 2), lax.rem(cz, 2), lax.rem(lax.div(cz, 2), 2), lax.div(cz, 4)]
    mates = [
        s + 1 - 2 * core,
        s + (1 - 2 * uppers[1]) * 2,
        s + (3 - 2 * cx) * 2,
        s + (1 - 2 * uppers[3]) * 8,
        s + (1 - 2 * uppers[4]) * 16,
    ]
    opposite = {"seq": s + (1 - 2 * uppers[5]) * 32}
    x_across = {"seq": s + (1 - 2 * uppers[2]) * 4}
    mates = [{"seq": m} for m in mates]
    is_top = cz >= 4
    is_source = jnp.logical_or(cz == 0, cz == 3)
    plane = lax.rem(s, 8)
    near = {"seq": jnp.where(cz == 0, 56, 32) + plane}
    far = {"seq": jnp.where(cz == 0, 48, 40) + plane}
    source = {"seq": jnp.where(cz < 6, 24, 0) + plane}

    def remote(src, dst, send, recv, device):
        return pltpu.make_async_remote_copy(
            src_ref=src, dst_ref=dst, send_sem=send, recv_sem=recv, device_id=device, device_id_type=MESH
        )

    locals_ = [
        pltpu.make_async_copy(x_ref, xg.at[y], loc.at[0]),
        pltpu.make_async_copy(wk_ref, wkv.at[:, pl.ds(0, SIZE)], loc.at[1]),
        pltpu.make_async_copy(wv_ref, wkv.at[:, pl.ds(SIZE, SIZE)], loc.at[2]),
        pltpu.make_async_copy(wq_ref, wq, loc.at[3]),
    ]
    own_out = pltpu.make_async_copy(wo_ref.at[:, pl.ds(pl.multiple_of(y * PART, PART), PART)], wown, loc.at[4])
    for c in locals_:
        c.start()

    @pl.when(jnp.logical_not(is_top))
    def _():
        bkt[BITS - 1] = jnp.zeros((HEADS * SIZE, SIZE), BF16)

    barrier = pltpu.get_barrier_semaphore()
    for peer in [to_right, to_left, to_across, opposite, x_across] + mates:
        pl.semaphore_signal(barrier, inc=1, device_id=peer, device_id_type=MESH)

    @pl.when(is_top)
    def _():
        pl.semaphore_signal(barrier, inc=1, device_id=source, device_id_type=MESH)

    pl.semaphore_wait(barrier, 5 + len(mates) + jnp.where(is_source, 2, 0))

    half = BLOCK // 2

    def own_rows(r, side):
        rows = pl.ds(pl.multiple_of(r * BLOCK, BLOCK), BLOCK)
        i = 2 * r + side
        return remote(x_ref.at[rows], xg.at[y, rows], tok_s.at[i], tok_r.at[i], to_left if side else to_right)

    def onward(r, side):
        rows = pl.ds(pl.multiple_of(r * BLOCK + side * half, half), half)
        i = 2 * BLOCKS + 2 * r + side
        owner = right if side else left
        return remote(xg.at[owner, rows], xg.at[owner, rows], tok_s.at[i], tok_r.at[i], to_left if side else to_right)

    wide_cols = pl.ds(pl.multiple_of(core * 512, 512), 512)
    cols_a = pl.ds(pl.multiple_of(core * 512, 256), 256)
    cols_b = pl.ds(pl.multiple_of(core * 512 + 256, 256), 256)
    piece = cx * 8 + cz

    def some_rows(start, count):
        return pl.ds(pl.multiple_of(start * 16, 16), count * 16)

    def spread_copy(i, rows, cols, device):
        part = wop.at[:, rows, cols]
        return remote(part, part, wo_s.at[i], wo_r.at[i], device)

    fetch = []
    for i, (peer, device) in enumerate(((right, to_right), (left, to_left), (across, to_across))):
        there = pl.ds(pl.multiple_of(peer * PART + core * 512, 512), 512)
        rows = some_rows(piece, 1)
        fetch.append(remote(wo_ref.at[rows, there], wop.at[i, rows, wide_cols], wo_s.at[i], wo_r.at[i], device))
    over_z = [
        spread_copy(3, some_rows(piece, 1), wide_cols, mates[3]),
        spread_copy(4, some_rows(piece - lax.rem(cz, 2), 2), wide_cols, mates[4]),
        spread_copy(5, some_rows(piece - lax.rem(cz, 4), 4), wide_cols, opposite),
    ]
    over_x = [
        spread_copy(6, some_rows(cx * 8, 8), cols_a, mates[1]),
        spread_copy(7, some_rows(cx * 8, 8), cols_b, mates[2]),
    ]
    over_x2 = [
        spread_copy(8, some_rows(lax.div(cx, 2) * 16, 16), cols_a, mates[2]),
        spread_copy(9, some_rows(cx * 8, 8), cols_b, mates[1]),
        spread_copy(10, some_rows((3 - cx) * 8, 8), cols_b, mates[1]),
    ]
    share = spread_copy(11, pl.ds(0, ROWS), wide_cols, mates[0])

    eighth = pl.ds(pl.multiple_of((core * 4 + cx) * 128, 128), 128)
    core_rows = pl.ds(pl.multiple_of(core * 512, 512), 512)
    kv_fetch = []
    for i, (peer, device) in enumerate(((right, to_right), (left, to_left), (across, to_across))):
        there = pl.ds(pl.multiple_of(peer * PART + (core * 4 + cx) * 128, 128), 128)
        kv_fetch.append(remote(wkv.at[there], wkp.at[i, eighth], kv_s.at[i], kv_r.at[i], device))
    kv_x = [
        remote(wkp.at[:, eighth], wkp.at[:, eighth], kv_s.at[3 + i], kv_r.at[3 + i], device)
        for i, device in enumerate((mates[1], mates[2], x_across))
    ]
    kv_share = remote(wkp.at[:, core_rows], wkp.at[:, core_rows], kv_s.at[6], kv_r.at[6], mates[0])
    kv_parts = [
        remote(psend.at[0], prec.at[1], kv_s.at[7], kv_r.at[7], to_left),
        remote(psend.at[1], prec.at[0], kv_s.at[8], kv_r.at[8], to_right),
        remote(psend.at[2], prec.at[2], kv_s.at[9], kv_r.at[9], to_across),
    ]
    locals_[1].wait()
    locals_[2].wait()
    for c in kv_fetch:
        c.start()

    half = BLOCK // 2

    def own_rows(r, side):
        rows = pl.ds(r * BLOCK, BLOCK)
        i = 2 * r + side
        return remote(x_ref.at[rows], xg.at[y, rows], tok_s.at[i], tok_r.at[i], to_left if side else to_right)

    def onward(r, side):
        rows = pl.ds(r * BLOCK + side * half, half)
        i = 2 * BLOCKS + 2 * r + side
        owner = right if side else left
        return remote(xg.at[owner, rows], xg.at[owner, rows], tok_s.at[i], tok_r.at[i], to_left if side else to_right)

    def send_own(r):
        own_rows(r, 0).start()
        own_rows(r, 1).start()

    def pass_on(r):
        for side in range(2):
            own_rows(r, side).wait_recv()
            onward(r, side).start()

    ldp[...] = jnp.zeros_like(ldp)
    ldp[0:HEADS, :] = ld_ref[...]
    row = lax.broadcasted_iota(jnp.int32, (ROWS, ROWS), 0)
    col = lax.broadcasted_iota(jnp.int32, (ROWS, ROWS), 1)
    lower = (row >= col).astype(F32).astype(BF16)
    upper_tri = (row <= col).astype(F32).astype(BF16)
    wide_row = lax.broadcasted_iota(jnp.int32, (BLOCK, HEADS * LEVELS), 0)
    wide_col = lax.broadcasted_iota(jnp.int32, (BLOCK, HEADS * LEVELS), 1)
    spread = (lax.div(wide_col, LEVELS) == wide_row).astype(F32).astype(BF16)
    level_of = lax.rem(lax.broadcasted_iota(jnp.int32, (8, HEADS * LEVELS), 1), LEVELS)
    spread_decay = sum(dot(lower, dot(p, spread).astype(BF16)) for p in split3(jnp.transpose(ldp[...])))
    d36[...] = spread_decay
    along = sum(dot(p, upper_tri) for p in split3(ldp[0:16, :]))
    dect[...] = along[0:8]
    for c in range(BLOCKS):
        last = (c + 1) * BLOCK - 1
        ends[c] = jnp.broadcast_to(dect[:, last : last + 1], (8, SIZE))
    gsend[0] = jnp.zeros((24, SIZE), F32)
    gsend[0, 0:8] = ends[BLOCKS - 1]
    gsend[0, 8:16, 0 : HEADS * LEVELS] = jnp.broadcast_to(d36[ROWS - 1 : ROWS, :], (8, HEADS * LEVELS))
    before = jnp.zeros((8, HEADS * LEVELS), F32)
    gap_off = jnp.zeros((8, HEADS * LEVELS), F32)
    decay_copies = []
    for bit in range(BITS - 1):
        up = uppers[bit].astype(F32)
        c = remote(gsend.at[bit], grecv.at[bit], dec_s.at[bit], dec_r.at[bit], mates[bit])
        c.start()
        if bit == 0:
            send_own(0)
            for d in fetch:
                d.start()
        if bit == 2:
            send_own(1)
            for d in kv_fetch:
                d.wait_recv()
            for d in kv_x:
                d.start()
            for d in fetch:
                d.wait_recv()
            over_z[0].start()
        if bit == 3:
            pass_on(0)
        if bit == 4:
            over_z[0].wait_recv()
            over_z[1].start()
        c.wait_recv()
        decay_copies.append(c)
        mine = gsend[bit]
        other = grecv[bit]
        coef[bit, 0] = up + (1.0 - up) * jnp.exp(other[0:8])
        coef[bit, 1] = up * jnp.exp(mine[0:8]) + (1.0 - up)
        gap_off = gap_off + jnp.where(level_of == 3 + bit, up * before + (1.0 - up) * NEVER, 0.0)
        before = before + up * other[8:16, 0 : HEADS * LEVELS]
        if bit < BITS - 2:
            gsend[bit + 1, 0:16] = mine[0:16] + other[0:16]
            gsend[bit + 1, 16:24] = mine[0:8]
        if bit == 2:
            third = other[16:24]
            fourth = other[0:8] - third
            side = uppers[1].astype(F32)
            pair[0] = side * jnp.exp(fourth) + (1.0 - side)
            pair[1] = side + (1.0 - side) * jnp.exp(third)
    up = uppers[BITS - 1].astype(F32)
    gap_off = gap_off + jnp.where(level_of == 3 + BITS - 1, up * before + (1.0 - up) * NEVER, 0.0)
    offs[...] = gap_off
    for c in (locals_[0], locals_[3]):
        c.wait()
    pass_on(1)
    for c in kv_x:
        c.wait_recv()
    kv_share.start()

    owners = (y, left, right, across)

    def project(r, weights, who=owners):
        rows = pl.ds(r * BLOCK, BLOCK)
        return sum(dot(xg[i, rows, :], weights[pl.ds(pl.multiple_of(i * PART, PART), PART), :]) for i in who)

    def keys_part(r):
        rows = pl.ds(r * BLOCK, BLOCK)
        part = project(r, wkv, owners[:3])
        onward(r, 0).wait_recv()
        onward(r, 1).wait_recv()
        finish_keys(r, part + project(r, wkv, owners[3:]))

    def keys_late(r):
        rows = pl.ds((r - EARLY) * BLOCK, BLOCK)
        both = project(r, wkv, owners[:1])
        for i in range(3):
            both = both + prec[i, rows, :].astype(F32)
        finish_keys(r, both)

    def finish_keys(r, both):
        rows = pl.ds(r * BLOCK, BLOCK)
        values = both[:, SIZE:].astype(BF16)
        kb[rows, :] = both[:, :SIZE].astype(BF16)
        vb[rows, :] = values
        k_t = jnp.transpose(both[:, :SIZE].astype(BF16).astype(F32))
        weight = jnp.exp(ends[r] - dect[:, r * BLOCK : (r + 1) * BLOCK])
        for h in range(HEADS):
            scaled = (k_t * weight[h : h + 1, :]).astype(BF16)
            sb[r, h * SIZE : (h + 1) * SIZE, :] = dot(scaled, values)

    def fade_of(c, before_c, h):
        return jnp.exp(ends[c] - ends[before_c])[h : h + 1, :]

    def query_part(r):
        rows = slice(r * BLOCK, (r + 1) * BLOCK)
        qb[rows, :] = project(r, wq).astype(BF16)
        weight = softplus(sum(dot_t(xg[i, rows, :], wl_ref[:, i * PART : (i + 1) * PART]) for i in range(4)))
        kind = level_of[0:1]
        off = offs[0:1, :]
        off = jnp.where(kind == 1, -d36[r * BLOCK - 1 : r * BLOCK, :] if r % 2 else NEVER, off)
        off = jnp.where(kind == 2, -d36[2 * BLOCK - 1 : 2 * BLOCK, :] if r >= 2 else NEVER, off)
        here = d36[rows, :]
        power = jnp.where(kind == 0, 0.0, here + off)
        factor = weight * jnp.exp(power)
        keys = kb[rows, :]
        values = vb[rows, :]
        inside_row = lax.broadcasted_iota(jnp.int32, (BLOCK, BLOCK), 0)
        inside_col = lax.broadcasted_iota(jnp.int32, (BLOCK, BLOCK), 1)
        causal = inside_row >= inside_col
        along_here = dect[:, rows]
        for h in range(HEADS):
            cols = slice(h * SIZE, (h + 1) * SIZE)
            query = qb[rows, cols]
            wide = query.astype(F32)
            scores = dot_t(query, keys)
            gap = here[:, h * LEVELS : h * LEVELS + 1] - along_here[h : h + 1, :]
            mixing = jnp.exp(jnp.where(causal, gap, NEVER)) * scores * factor[:, h * LEVELS : h * LEVELS + 1]
            total = dot(mixing.astype(BF16), values)
            if r % 2:
                near_query = (wide * factor[:, h * LEVELS + 1 : h * LEVELS + 2]).astype(BF16)
                total = total + dot(near_query, sb[r - 1, cols, :].astype(BF16))
            if r >= 2:
                late_query = (wide * factor[:, h * LEVELS + 2 : h * LEVELS + 3]).astype(BF16)
                total = total + dot(late_query, sb16[cols, :])
            acc[rows, cols] = total
            for bit in range(BITS):
                at = h * LEVELS + 3 + bit
                qs[bit, rows, cols] = (wide * factor[:, at : at + 1]).astype(BF16)

    def pair_sum():
        for h in range(HEADS):
            cols = slice(h * SIZE, (h + 1) * SIZE)
            sb16[cols, :] = (sb[1, cols, :] + fade_of(1, 0, h) * sb[0, cols, :]).astype(BF16)

    keys_part(0)
    kv_share.wait_recv()
    for i in (2, 0, 1):
        psend[i] = dot(xg[y, EARLY * BLOCK :, :], wkp[i]).astype(BF16)
        kv_parts[i].start()
    over_z[1].wait_recv()
    over_z[2].start()
    keys_part(1)
    pair_sum()
    query_part(0)
    query_part(1)
    send_own(2)
    for c in kv_parts:
        c.wait_recv()
    send_own(3)
    for r in range(EARLY, BLOCKS):
        keys_late(r)
    for h in range(HEADS):
        cols = slice(h * SIZE, (h + 1) * SIZE)
        first = sb[1, cols, :] + fade_of(1, 0, h) * sb[0, cols, :]
        second = sb[3, cols, :] + fade_of(3, 2, h) * sb[2, cols, :]
        whole = second + fade_of(3, 1, h) * first
        run[cols, :] = whole
        ssend[0, cols, :] = whole.astype(BF16)

    last_bit = BITS - 1

    def head_rows(wave):
        return pl.ds(pl.multiple_of((2 * wave + core) * SIZE, SIZE), SIZE)

    def state_copy(bit, wave):
        rows = pl.ds(2 * wave * SIZE, 2 * SIZE) if bit == 0 else head_rows(wave)
        i = 2 * bit + wave
        return remote(ssend.at[bit, rows], bkt.at[bit, rows], st_s.at[i], st_r.at[i], mates[bit])

    def top_copy(wave, device, place):
        rows = head_rows(wave)
        i = 2 * last_bit + wave
        return remote(ssend.at[last_bit, rows], bkt.at[last_bit, rows], st_s.at[i + 2 * place], st_r.at[i], device)

    def hand_over(bit, wave):
        rows = head_rows(wave)
        i = 2 * bit + wave
        return remote(bkt.at[bit, rows], bkt.at[bit, rows], fw_s.at[i], fw_r.at[i], mates[0])

    for wave in range(2):
        state_copy(0, wave).start()
    own_out.start()

    def take(bit):
        for h in range(HEADS):
            cols = slice(h * SIZE, (h + 1) * SIZE)
            acc[:, cols] += dot(qs[bit, :, cols], bkt[bit, cols, :])

    def corner(wave, third):
        rows = head_rows(wave)
        if third:
            return remote(ssend.at[1, rows], xin.at[0, rows], st_s.at[4 + wave], st_r.at[4 + wave], mates[2])
        return remote(ssend.at[1, rows], xin.at[1, rows], xs.at[wave], xr.at[wave], x_across)

    def scale(row, wave):
        return row[pl.ds(2 * wave + core, 1), :]

    def merge(bit, wave, other):
        one = head_rows(wave)
        return scale(coef.at[bit, 0], wave) * run[one, :] + scale(coef.at[bit, 1], wave) * other

    for wave in range(2):
        one = head_rows(wave)
        state_copy(0, wave).wait_recv()
        merged = merge(0, wave, bkt[0, one, :].astype(F32))
        run[one, :] = merged
        ssend[1, one, :] = merged.astype(BF16)
        corner(wave, False).start()
        state_copy(1, wave).start()
        corner(wave, True).start()
    for wave in range(2):
        one = head_rows(wave)
        state_copy(1, wave).wait_recv()
        corner(wave, True).wait_recv()
        corner(wave, False).wait_recv()
        run[one, :] = merge(1, wave, bkt[1, one, :].astype(F32))
        second = scale(pair.at[0], wave) * xin[0, one, :].astype(F32) + scale(pair.at[1], wave) * xin[1, one, :].astype(F32)
        merged = merge(2, wave, second)
        run[one, :] = merged
        ssend[3, one, :] = merged.astype(BF16)
        state_copy(3, wave).start()
        bkt[2, one, :] = second.astype(BF16)
        hand_over(1, wave).start()
        hand_over(2, wave).start()
    over_z[2].wait_recv()
    for c in over_x:
        c.start()
    pass_on(2)
    for wave in range(2):
        one = head_rows(wave)
        state_copy(3, wave).wait_recv()
        merged = merge(3, wave, bkt[3, one, :].astype(F32))
        run[one, :] = merged
        ssend[4, one, :] = merged.astype(BF16)
        state_copy(4, wave).start()
        hand_over(3, wave).start()
    pass_on(3)
    for wave in range(2):
        one = head_rows(wave)
        state_copy(4, wave).wait_recv()
        ssend[last_bit, one, :] = merge(4, wave, bkt[4, one, :].astype(F32)).astype(BF16)

        @pl.when(is_source)
        def _(wave=wave):
            top_copy(wave, near, 0).start()
            top_copy(wave, far, 1).start()

        hand_over(4, wave).start()
    for c in over_x:
        c.wait_recv()
    for c in over_x2:
        c.start()
    for r in range(2, BLOCKS):
        onward(r, 0).wait_recv()
        onward(r, 1).wait_recv()
        query_part(r)

    many = ROWS // 2

    def own_normed(u, side):
        part = ng.at[y, u // 2, pl.ds(u % 2 * many, many)]
        i = 2 * u + side
        return remote(part, part, nm_s.at[i], nm_r.at[i], to_left if side else to_right)

    def onward_normed(u, side):
        part = ng.at[right if side else left, u // 2, pl.ds(u % 2 * many + side * BLOCK, BLOCK)]
        i = 8 + 2 * u + side
        return remote(part, part, nm_s.at[i], nm_r.at[i], to_left if side else to_right)

    for wave in range(2):

        @pl.when(is_top)
        def _(wave=wave):
            top_copy(wave, source, 0).wait_recv()
            hand_over(last_bit, wave).start()

    for bit in range(last_bit):
        if bit > 0:
            for wave in range(2):
                hand_over(bit, wave).wait_recv()
        take(bit)
    for wave in range(2):

        @pl.when(is_top)
        def _(wave=wave):
            hand_over(last_bit, wave).wait_recv()

        for part in range(2):
            rows = slice(part * many, (part + 1) * many)
            for i in range(2):
                h = 2 * wave + i
                cols = slice(h * SIZE, (h + 1) * SIZE)
                value = acc[rows, cols] + dot(qs[last_bit, rows, cols], bkt[last_bit, cols, :])
                mean = jnp.mean(value * value, axis=-1, keepdims=True)
                ng[y, wave, rows, i * SIZE : (i + 1) * SIZE] = (value * lax.rsqrt(mean + 1e-05)).astype(BF16)
            own_normed(2 * wave + part, 0).start()
            own_normed(2 * wave + part, 1).start()

    def pass_normed(u):
        for side in range(2):
            own_normed(u, side).wait_recv()
            onward_normed(u, side).start()

    pass_normed(0)
    for c in over_x2:
        c.wait_recv()
    share.start()
    pass_normed(1)
    pass_normed(2)
    own_out.wait()
    share.wait_recv()

    def place(u):
        wave = u // 2
        return wave, slice(u % 2 * many, (u % 2 + 1) * many), slice(wave * 256, (wave + 1) * 256)

    for u in range(4):
        if u == 2:
            pass_normed(3)
        wave, rows, depth = place(u)
        product = dot(ng[y, wave, rows, :], wown[depth, :])
        product = product + dot(ng[left, wave, rows, :], wop[0, depth, :])
        product = product + dot(ng[right, wave, rows, :], wop[1, depth, :])
        pacc[wave, rows, :] = product
    for u in range(4):
        onward_normed(u, 0).wait_recv()
        onward_normed(u, 1).wait_recv()
        wave, rows, depth = place(u)
        product = pacc[wave, rows, :] + dot(ng[across, wave, rows, :], wop[2, depth, :])
        if wave == 0:
            pacc[0, rows, :] = product
        else:
            out_ref[rows, :] = (pacc[0, rows, :] + product).astype(BF16)

    for r in range(BLOCKS):
        for side in range(2):
            own_rows(r, side).wait_send()
            onward(r, side).wait_send()
            own_normed(r, side).wait_send()
            onward_normed(r, side).wait_send()
    for c in decay_copies + kv_fetch + kv_x + [kv_share] + kv_parts + fetch + over_z + over_x + over_x2 + [share]:
        c.wait_send()
    for wave in range(2):
        corner(wave, True).wait_send()
        corner(wave, False).wait_send()
        for bit in range(last_bit):
            if bit != 2:
                state_copy(bit, wave).wait_send()
            if bit > 0:
                hand_over(bit, wave).wait_send()

        @pl.when(is_source)
        def _(wave=wave):
            top_copy(wave, near, 0).wait_send()
            top_copy(wave, far, 1).wait_send()

        @pl.when(is_top)
        def _(wave=wave):
            hand_over(last_bit, wave).wait_send()


def body(tokens, log_decay, w_query, w_key, w_value, w_level, w_out):
    hbm = pl.BlockSpec(memory_space=pl.ANY)
    vmem = pl.BlockSpec(memory_space=pltpu.VMEM)
    dma = pltpu.SemaphoreType.DMA
    wide = HEADS * LEVELS
    return pl.pallas_call(
        kernel,
        name="layer",
        out_shape=pltpu.VMEM((ROWS, PART), BF16),
        in_specs=[hbm, vmem, hbm, hbm, hbm, vmem, hbm],
        out_specs=vmem,
        scratch_shapes=[
            pltpu.VMEM((4, ROWS, PART), BF16),
            pltpu.VMEM((4 * PART, HEADS * SIZE), BF16),
            pltpu.VMEM((4 * PART, 2 * SIZE), BF16),
            pltpu.VMEM((3, PART, 2 * SIZE), BF16),
            pltpu.VMEM((3, LATE, 2 * SIZE), BF16),
            pltpu.VMEM((3, LATE, 2 * SIZE), BF16),
            pltpu.VMEM((HEADS * SIZE, PART), BF16),
            pltpu.VMEM((3, HEADS * SIZE, PART), BF16),
            pltpu.VMEM((4, 2, ROWS, 2 * SIZE), BF16),
            pltpu.VMEM((2, ROWS, PART), F32),
            pltpu.VMEM((SIZE, ROWS), F32),
            pltpu.VMEM((ROWS, wide), F32),
            pltpu.VMEM((8, ROWS), F32),
            pltpu.VMEM((BLOCKS, 8, SIZE), F32),
            pltpu.VMEM((8, wide), F32),
            pltpu.VMEM((BITS - 1, 24, SIZE), F32),
            pltpu.VMEM((BITS - 1, 24, SIZE), F32),
            pltpu.VMEM((BITS - 1, 2, 8, SIZE), F32),
            pltpu.VMEM((2, 8, SIZE), F32),
            pltpu.VMEM((2, HEADS * SIZE, SIZE), BF16),
            pltpu.VMEM((ROWS, HEADS * SIZE), BF16),
            pltpu.VMEM((ROWS, SIZE), BF16),
            pltpu.VMEM((ROWS, SIZE), BF16),
            pltpu.VMEM((ROWS, HEADS * SIZE), F32),
            pltpu.VMEM((BITS, ROWS, HEADS * SIZE), BF16),
            pltpu.VMEM((BLOCKS, HEADS * SIZE, SIZE), F32),
            pltpu.VMEM((HEADS * SIZE, SIZE), BF16),
            pltpu.VMEM((HEADS * SIZE, SIZE), F32),
            pltpu.VMEM((BITS, HEADS * SIZE, SIZE), BF16),
            pltpu.VMEM((BITS, HEADS * SIZE, SIZE), BF16),
            dma((4 * BLOCKS,)), dma((4 * BLOCKS,)),
            dma((BITS - 1,)), dma((BITS - 1,)),
            dma((2 * BITS + 2,)), dma((2 * BITS,)),
            dma((2,)), dma((2,)),
            dma((2 * BITS,)), dma((2 * BITS,)),
            dma((12,)), dma((12,)),
            dma((10,)), dma((10,)),
            dma((4 * BLOCKS,)), dma((4 * BLOCKS,)),
            dma((5,)),
        ],
        compiler_params=pltpu.CompilerParams(
            collective_id=0, has_side_effects=True, vmem_limit_bytes=56 << 20
        ),
        cost_estimate=pl.CostEstimate(flops=7_000_000_000, bytes_accessed=14_000_000, transcendentals=400_000),
    )(tokens, log_decay.T, w_query, w_key, w_value, w_level.T, w_out)


def solution(mesh):
    in_specs = (
        P("seq", "tp"),
        P("seq", "tp"),
        P(None, "tp"),
        P(None, "tp"),
        P(None, "tp"),
        P(None, "tp"),
        P("tp", None),
    )
    return jax.shard_map(
        body, mesh=mesh, in_specs=in_specs, out_specs=P("seq", "tp"), check_vma=False
    )
```

```python
import jax
import jax.numpy as jnp
from jax import lax
from jax.experimental import pallas as pl
from jax.experimental.pallas import tpu as pltpu
from jax.sharding import PartitionSpec as P

BLOCK = 128
F32 = jnp.float32
BF16 = jnp.bfloat16
MESH = pl.DeviceIdType.MESH
NEVER = -1e30
HEADS = 4
SIZE = 128
LEVELS = 9
ROWS = 512
BLOCKS = ROWS // BLOCK
PART = 1024
BITS = 6
EARLY = 2
LATE = ROWS - EARLY * BLOCK


def dot(a, b):
    return jnp.dot(a, b, preferred_element_type=F32)


def dot_t(a, b):
    return lax.dot_general(a, b, (((1,), (1,)), ((), ())), preferred_element_type=F32)


def split3(wide):
    high = wide.astype(BF16)
    rest = wide - high.astype(F32)
    middle = rest.astype(BF16)
    low = (rest - middle.astype(F32)).astype(BF16)
    return high, middle, low


def softplus(x):
    return jnp.maximum(x, 0.0) + jnp.log1p(jnp.exp(-jnp.abs(x)))


def kernel(
    x_ref, ld_ref, wq_ref, wk_ref, wv_ref, wl_ref, wo_ref, out_ref,
    xg, wq, wkv, wkp, psend, prec, wown, wop, ng, pacc,
    ldp, d36, dect, ends, offs, gsend, grecv, coef, pair, xin,
    qb, kb, vb, acc, qs, sb, sb16, run, ssend, bkt,
    tok_s, tok_r, dec_s, dec_r, st_s, st_r, xs, xr, fw_s, fw_r, wo_s, wo_r, kv_s, kv_r, nm_s, nm_r, ready, loc,
):
    y = lax.axis_index("tp")
    s = lax.axis_index("seq")
    core = lax.rem(s, 2)
    cx = lax.rem(lax.div(s, 2), 4)
    cz = lax.div(s, 8)
    right, left, across = lax.rem(y + 1, 4), lax.rem(y + 3, 4), lax.rem(y + 2, 4)
    to_right, to_left, to_across = {"tp": right}, {"tp": left}, {"tp": across}
    uppers = [core, lax.rem(cx, 2), lax.div(cx, 2), lax.rem(cz, 2), lax.rem(lax.div(cz, 2), 2), lax.div(cz, 4)]
    mates = [
        s + 1 - 2 * core,
        s + (1 - 2 * uppers[1]) * 2,
        s + (3 - 2 * cx) * 2,
        s + (1 - 2 * uppers[3]) * 8,
        s + (1 - 2 * uppers[4]) * 16,
    ]
    opposite = {"seq": s + (1 - 2 * uppers[5]) * 32}
    x_across = {"seq": s + (1 - 2 * uppers[2]) * 4}
    mates = [{"seq": m} for m in mates]
    is_top = cz >= 4
    is_source = jnp.logical_or(cz == 0, cz == 3)
    plane = lax.rem(s, 8)
    near = {"seq": jnp.where(cz == 0, 56, 32) + plane}
    far = {"seq": jnp.where(cz == 0, 48, 40) + plane}
    source = {"seq": jnp.where(cz < 6, 24, 0) + plane}

    def remote(src, dst, send, recv, device):
        return pltpu.make_async_remote_copy(
            src_ref=src, dst_ref=dst, send_sem=send, recv_sem=recv, device_id=device, device_id_type=MESH
        )

    locals_ = [
        pltpu.make_async_copy(x_ref, xg.at[y], loc.at[0]),
        pltpu.make_async_copy(wk_ref, wkv.at[:, pl.ds(0, SIZE)], loc.at[1]),
        pltpu.make_async_copy(wv_ref, wkv.at[:, pl.ds(SIZE, SIZE)], loc.at[2]),
        pltpu.make_async_copy(wq_ref, wq, loc.at[3]),
    ]
    own_out = pltpu.make_async_copy(wo_ref.at[:, pl.ds(pl.multiple_of(y * PART, PART), PART)], wown, loc.at[4])
    for c in locals_:
        c.start()

    @pl.when(jnp.logical_not(is_top))
    def _():
        bkt[BITS - 1] = jnp.zeros((HEADS * SIZE, SIZE), BF16)

    barrier = pltpu.get_barrier_semaphore()
    in_half = [to_right, to_left, to_across, x_across] + mates
    for peer in in_half:
        pl.semaphore_signal(barrier, inc=1, device_id=peer, device_id_type=MESH)

    @pl.when(jnp.logical_not(is_top))
    def _():
        pl.semaphore_signal(barrier, inc=1, device_id=opposite, device_id_type=MESH)

    @pl.when(is_source)
    def _():
        pl.semaphore_signal(barrier, inc=1, device_id=near, device_id_type=MESH)
        pl.semaphore_signal(barrier, inc=1, device_id=far, device_id_type=MESH)

    pl.semaphore_wait(barrier, len(in_half) + jnp.where(is_top, 2, 0))

    @pl.when(is_top)
    def _():
        pl.semaphore_signal(ready.at[0], inc=1, device_id=opposite, device_id_type=MESH)
        pl.semaphore_signal(ready.at[1], inc=1, device_id=source, device_id_type=MESH)

    wide_cols = pl.ds(pl.multiple_of(core * 512, 512), 512)
    cols_a = pl.ds(pl.multiple_of(core * 512, 256), 256)
    cols_b = pl.ds(pl.multiple_of(core * 512 + 256, 256), 256)
    piece = cx * 8 + cz

    def some_rows(start, count):
        return pl.ds(pl.multiple_of(start * 16, 16), count * 16)

    def spread_copy(i, rows, cols, device):
        part = wop.at[:, rows, cols]
        return remote(part, part, wo_s.at[i], wo_r.at[i], device)

    fetch = []
    for i, (peer, device) in enumerate(((right, to_right), (left, to_left), (across, to_across))):
        there = pl.ds(pl.multiple_of(peer * PART + core * 512, 512), 512)
        rows = some_rows(piece, 1)
        fetch.append(remote(wo_ref.at[rows, there], wop.at[i, rows, wide_cols], wo_s.at[i], wo_r.at[i], device))
    over_z = [
        spread_copy(3, some_rows(piece, 1), wide_cols, mates[3]),
        spread_copy(4, some_rows(piece - lax.rem(cz, 2), 2), wide_cols, mates[4]),
        spread_copy(5, some_rows(piece - lax.rem(cz, 4), 4), wide_cols, opposite),
    ]
    over_x = [
        spread_copy(6, some_rows(cx * 8, 8), cols_a, mates[1]),
        spread_copy(7, some_rows(cx * 8, 8), cols_b, mates[2]),
    ]
    over_x2 = [
        spread_copy(8, some_rows(lax.div(cx, 2) * 16, 16), cols_a, mates[2]),
        spread_copy(9, some_rows(cx * 8, 8), cols_b, mates[1]),
        spread_copy(10, some_rows((3 - cx) * 8, 8), cols_b, mates[1]),
    ]
    share = spread_copy(11, pl.ds(0, ROWS), wide_cols, mates[0])

    eighth = pl.ds(pl.multiple_of((core * 4 + cx) * 128, 128), 128)
    core_rows = pl.ds(pl.multiple_of(core * 512, 512), 512)
    kv_fetch = []
    for i, (peer, device) in enumerate(((right, to_right), (left, to_left), (across, to_across))):
        there = pl.ds(pl.multiple_of(peer * PART + (core * 4 + cx) * 128, 128), 128)
        kv_fetch.append(remote(wkv.at[there], wkp.at[i, eighth], kv_s.at[i], kv_r.at[i], device))
    kv_x = [
        remote(wkp.at[:, eighth], wkp.at[:, eighth], kv_s.at[3 + i], kv_r.at[3 + i], device)
        for i, device in enumerate((mates[1], mates[2], x_across))
    ]
    kv_share = remote(wkp.at[:, core_rows], wkp.at[:, core_rows], kv_s.at[6], kv_r.at[6], mates[0])
    kv_parts = [
        remote(psend.at[0], prec.at[1], kv_s.at[7], kv_r.at[7], to_left),
        remote(psend.at[1], prec.at[0], kv_s.at[8], kv_r.at[8], to_right),
        remote(psend.at[2], prec.at[2], kv_s.at[9], kv_r.at[9], to_across),
    ]
    locals_[1].wait()
    locals_[2].wait()
    for c in kv_fetch:
        c.start()

    half = BLOCK // 2

    def own_rows(r, side):
        rows = pl.ds(r * BLOCK, BLOCK)
        i = 2 * r + side
        return remote(x_ref.at[rows], xg.at[y, rows], tok_s.at[i], tok_r.at[i], to_left if side else to_right)

    def onward(r, side):
        rows = pl.ds(r * BLOCK + side * half, half)
        i = 2 * BLOCKS + 2 * r + side
        owner = right if side else left
        return remote(xg.at[owner, rows], xg.at[owner, rows], tok_s.at[i], tok_r.at[i], to_left if side else to_right)

    def send_own(r):
        own_rows(r, 0).start()
        own_rows(r, 1).start()

    def pass_on(r):
        for side in range(2):
            own_rows(r, side).wait_recv()
            onward(r, side).start()

    ldp[...] = jnp.zeros_like(ldp)
    ldp[0:HEADS, :] = ld_ref[...]
    row = lax.broadcasted_iota(jnp.int32, (ROWS, ROWS), 0)
    col = lax.broadcasted_iota(jnp.int32, (ROWS, ROWS), 1)
    lower = (row >= col).astype(F32).astype(BF16)
    upper_tri = (row <= col).astype(F32).astype(BF16)
    wide_row = lax.broadcasted_iota(jnp.int32, (BLOCK, HEADS * LEVELS), 0)
    wide_col = lax.broadcasted_iota(jnp.int32, (BLOCK, HEADS * LEVELS), 1)
    spread = (lax.div(wide_col, LEVELS) == wide_row).astype(F32).astype(BF16)
    level_of = lax.rem(lax.broadcasted_iota(jnp.int32, (8, HEADS * LEVELS), 1), LEVELS)
    spread_decay = sum(dot(lower, dot(p, spread).astype(BF16)) for p in split3(jnp.transpose(ldp[...])))
    d36[...] = spread_decay
    along = sum(dot(p, upper_tri) for p in split3(ldp[0:16, :]))
    dect[...] = along[0:8]
    for c in range(BLOCKS):
        last = (c + 1) * BLOCK - 1
        ends[c] = jnp.broadcast_to(dect[:, last : last + 1], (8, SIZE))
    gsend[0] = jnp.zeros((24, SIZE), F32)
    gsend[0, 0:8] = ends[BLOCKS - 1]
    gsend[0, 8:16, 0 : HEADS * LEVELS] = jnp.broadcast_to(d36[ROWS - 1 : ROWS, :], (8, HEADS * LEVELS))
    before = jnp.zeros((8, HEADS * LEVELS), F32)
    gap_off = jnp.zeros((8, HEADS * LEVELS), F32)
    decay_copies = []
    for bit in range(BITS - 1):
        up = uppers[bit].astype(F32)
        c = remote(gsend.at[bit], grecv.at[bit], dec_s.at[bit], dec_r.at[bit], mates[bit])
        c.start()
        if bit == 0:
            send_own(0)
            for d in fetch:
                d.start()
        if bit == 2:
            send_own(1)
            for d in kv_fetch:
                d.wait_recv()
            for d in kv_x:
                d.start()
            for d in fetch:
                d.wait_recv()
            over_z[0].start()
        if bit == 3:
            pass_on(0)
        if bit == 4:
            over_z[0].wait_recv()
            over_z[1].start()
        c.wait_recv()
        decay_copies.append(c)
        mine = gsend[bit]
        other = grecv[bit]
        coef[bit, 0] = up + (1.0 - up) * jnp.exp(other[0:8])
        coef[bit, 1] = up * jnp.exp(mine[0:8]) + (1.0 - up)
        gap_off = gap_off + jnp.where(level_of == 3 + bit, up * before + (1.0 - up) * NEVER, 0.0)
        before = before + up * other[8:16, 0 : HEADS * LEVELS]
        if bit < BITS - 2:
            gsend[bit + 1, 0:16] = mine[0:16] + other[0:16]
            gsend[bit + 1, 16:24] = mine[0:8]
        if bit == 2:
            third = other[16:24]
            fourth = other[0:8] - third
            side = uppers[1].astype(F32)
            pair[0] = side * jnp.exp(fourth) + (1.0 - side)
            pair[1] = side + (1.0 - side) * jnp.exp(third)
    up = uppers[BITS - 1].astype(F32)
    gap_off = gap_off + jnp.where(level_of == 3 + BITS - 1, up * before + (1.0 - up) * NEVER, 0.0)
    offs[...] = gap_off
    for c in (locals_[0], locals_[3]):
        c.wait()
    pass_on(1)
    for c in kv_x:
        c.wait_recv()
    kv_share.start()

    owners = (y, left, right, across)

    def project(r, weights, who=owners):
        rows = pl.ds(r * BLOCK, BLOCK)
        return sum(dot(xg[i, rows, :], weights[pl.ds(pl.multiple_of(i * PART, PART), PART), :]) for i in who)

    def keys_part(r):
        rows = pl.ds(r * BLOCK, BLOCK)
        part = project(r, wkv, owners[:3])
        onward(r, 0).wait_recv()
        onward(r, 1).wait_recv()
        finish_keys(r, part + project(r, wkv, owners[3:]))

    def keys_late(r):
        rows = pl.ds((r - EARLY) * BLOCK, BLOCK)
        both = project(r, wkv, owners[:1])
        for i in range(3):
            both = both + prec[i, rows, :].astype(F32)
        finish_keys(r, both)

    def finish_keys(r, both):
        rows = pl.ds(r * BLOCK, BLOCK)
        values = both[:, SIZE:].astype(BF16)
        kb[rows, :] = both[:, :SIZE].astype(BF16)
        vb[rows, :] = values
        k_t = jnp.transpose(both[:, :SIZE].astype(BF16).astype(F32))
        weight = jnp.exp(ends[r] - dect[:, r * BLOCK : (r + 1) * BLOCK])
        for h in range(HEADS):
            scaled = (k_t * weight[h : h + 1, :]).astype(BF16)
            sb[r, h * SIZE : (h + 1) * SIZE, :] = dot(scaled, values)

    def fade_of(c, before_c, h):
        return jnp.exp(ends[c] - ends[before_c])[h : h + 1, :]

    def query_part(r):
        rows = slice(r * BLOCK, (r + 1) * BLOCK)
        qb[rows, :] = project(r, wq).astype(BF16)
        weight = softplus(sum(dot_t(xg[i, rows, :], wl_ref[:, i * PART : (i + 1) * PART]) for i in range(4)))
        kind = level_of[0:1]
        off = offs[0:1, :]
        off = jnp.where(kind == 1, -d36[r * BLOCK - 1 : r * BLOCK, :] if r % 2 else NEVER, off)
        off = jnp.where(kind == 2, -d36[2 * BLOCK - 1 : 2 * BLOCK, :] if r >= 2 else NEVER, off)
        here = d36[rows, :]
        power = jnp.where(kind == 0, 0.0, here + off)
        factor = weight * jnp.exp(power)
        keys = kb[rows, :]
        values = vb[rows, :]
        inside_row = lax.broadcasted_iota(jnp.int32, (BLOCK, BLOCK), 0)
        inside_col = lax.broadcasted_iota(jnp.int32, (BLOCK, BLOCK), 1)
        causal = inside_row >= inside_col
        along_here = dect[:, rows]
        for h in range(HEADS):
            cols = slice(h * SIZE, (h + 1) * SIZE)
            query = qb[rows, cols]
            wide = query.astype(F32)
            scores = dot_t(query, keys)
            gap = here[:, h * LEVELS : h * LEVELS + 1] - along_here[h : h + 1, :]
            mixing = jnp.exp(jnp.where(causal, gap, NEVER)) * scores * factor[:, h * LEVELS : h * LEVELS + 1]
            total = dot(mixing.astype(BF16), values)
            if r % 2:
                near_query = (wide * factor[:, h * LEVELS + 1 : h * LEVELS + 2]).astype(BF16)
                total = total + dot(near_query, sb[r - 1, cols, :].astype(BF16))
            if r >= 2:
                late_query = (wide * factor[:, h * LEVELS + 2 : h * LEVELS + 3]).astype(BF16)
                total = total + dot(late_query, sb16[cols, :])
            acc[rows, cols] = total
            for bit in range(BITS):
                at = h * LEVELS + 3 + bit
                qs[bit, rows, cols] = (wide * factor[:, at : at + 1]).astype(BF16)

    def pair_sum():
        for h in range(HEADS):
            cols = slice(h * SIZE, (h + 1) * SIZE)
            sb16[cols, :] = (sb[1, cols, :] + fade_of(1, 0, h) * sb[0, cols, :]).astype(BF16)

    keys_part(0)
    kv_share.wait_recv()
    for i in (2, 0, 1):
        psend[i] = dot(xg[y, EARLY * BLOCK :, :], wkp[i]).astype(BF16)
        kv_parts[i].start()
    over_z[1].wait_recv()

    @pl.when(jnp.logical_not(is_top))
    def _():
        pl.semaphore_wait(ready.at[0], 1)

    over_z[2].start()
    keys_part(1)
    pair_sum()
    query_part(0)
    query_part(1)
    send_own(2)
    for c in kv_parts:
        c.wait_recv()
    send_own(3)
    for r in range(EARLY, BLOCKS):
        keys_late(r)
    for h in range(HEADS):
        cols = slice(h * SIZE, (h + 1) * SIZE)
        first = sb[1, cols, :] + fade_of(1, 0, h) * sb[0, cols, :]
        second = sb[3, cols, :] + fade_of(3, 2, h) * sb[2, cols, :]
        whole = second + fade_of(3, 1, h) * first
        run[cols, :] = whole
        ssend[0, cols, :] = whole.astype(BF16)

    last_bit = BITS - 1

    def head_rows(wave):
        return pl.ds(pl.multiple_of((2 * wave + core) * SIZE, SIZE), SIZE)

    def state_copy(bit, wave):
        rows = pl.ds(2 * wave * SIZE, 2 * SIZE) if bit == 0 else head_rows(wave)
        i = 2 * bit + wave
        return remote(ssend.at[bit, rows], bkt.at[bit, rows], st_s.at[i], st_r.at[i], mates[bit])

    def top_copy(wave, device, place):
        rows = head_rows(wave)
        i = 2 * last_bit + wave
        return remote(ssend.at[last_bit, rows], bkt.at[last_bit, rows], st_s.at[i + 2 * place], st_r.at[i], device)

    def hand_over(bit, wave):
        rows = head_rows(wave)
        i = 2 * bit + wave
        return remote(bkt.at[bit, rows], bkt.at[bit, rows], fw_s.at[i], fw_r.at[i], mates[0])

    for wave in range(2):
        state_copy(0, wave).start()
    own_out.start()

    def take(bit):
        for h in range(HEADS):
            cols = slice(h * SIZE, (h + 1) * SIZE)
            acc[:, cols] += dot(qs[bit, :, cols], bkt[bit, cols, :])

    def corner(wave, third):
        rows = head_rows(wave)
        if third:
            return remote(ssend.at[1, rows], xin.at[0, rows], st_s.at[4 + wave], st_r.at[4 + wave], mates[2])
        return remote(ssend.at[1, rows], xin.at[1, rows], xs.at[wave], xr.at[wave], x_across)

    def scale(row, wave):
        return row[pl.ds(2 * wave + core, 1), :]

    def merge(bit, wave, other):
        one = head_rows(wave)
        return scale(coef.at[bit, 0], wave) * run[one, :] + scale(coef.at[bit, 1], wave) * other

    for wave in range(2):
        one = head_rows(wave)
        state_copy(0, wave).wait_recv()
        merged = merge(0, wave, bkt[0, one, :].astype(F32))
        run[one, :] = merged
        ssend[1, one, :] = merged.astype(BF16)
        corner(wave, False).start()
        state_copy(1, wave).start()
        corner(wave, True).start()
    for wave in range(2):
        one = head_rows(wave)
        state_copy(1, wave).wait_recv()
        corner(wave, True).wait_recv()
        corner(wave, False).wait_recv()
        run[one, :] = merge(1, wave, bkt[1, one, :].astype(F32))
        second = scale(pair.at[0], wave) * xin[0, one, :].astype(F32) + scale(pair.at[1], wave) * xin[1, one, :].astype(F32)
        merged = merge(2, wave, second)
        run[one, :] = merged
        ssend[3, one, :] = merged.astype(BF16)
        state_copy(3, wave).start()
        bkt[2, one, :] = second.astype(BF16)
        hand_over(1, wave).start()
        hand_over(2, wave).start()
    over_z[2].wait_recv()
    for c in over_x:
        c.start()
    pass_on(2)
    for wave in range(2):
        one = head_rows(wave)
        state_copy(3, wave).wait_recv()
        merged = merge(3, wave, bkt[3, one, :].astype(F32))
        run[one, :] = merged
        ssend[4, one, :] = merged.astype(BF16)
        state_copy(4, wave).start()
        hand_over(3, wave).start()
    pass_on(3)
    for wave in range(2):
        one = head_rows(wave)
        state_copy(4, wave).wait_recv()
        ssend[last_bit, one, :] = merge(4, wave, bkt[4, one, :].astype(F32)).astype(BF16)

        @pl.when(is_source)
        def _(wave=wave):
            if wave == 0:
                pl.semaphore_wait(ready.at[1], 2)
            top_copy(wave, near, 0).start()
            top_copy(wave, far, 1).start()

        hand_over(4, wave).start()
    for c in over_x:
        c.wait_recv()
    for c in over_x2:
        c.start()
    for r in range(2, BLOCKS):
        onward(r, 0).wait_recv()
        onward(r, 1).wait_recv()
        query_part(r)

    many = ROWS // 2

    def own_normed(u, side):
        part = ng.at[y, u // 2, pl.ds(u % 2 * many, many)]
        i = 2 * u + side
        return remote(part, part, nm_s.at[i], nm_r.at[i], to_left if side else to_right)

    def onward_normed(u, side):
        part = ng.at[right if side else left, u // 2, pl.ds(u % 2 * many + side * BLOCK, BLOCK)]
        i = 8 + 2 * u + side
        return remote(part, part, nm_s.at[i], nm_r.at[i], to_left if side else to_right)

    for wave in range(2):

        @pl.when(is_top)
        def _(wave=wave):
            top_copy(wave, source, 0).wait_recv()
            hand_over(last_bit, wave).start()

    for bit in range(last_bit):
        if bit > 0:
            for wave in range(2):
                hand_over(bit, wave).wait_recv()
        take(bit)
    for wave in range(2):

        @pl.when(is_top)
        def _(wave=wave):
            hand_over(last_bit, wave).wait_recv()

        for part in range(2):
            rows = slice(part * many, (part + 1) * many)
            for i in range(2):
                h = 2 * wave + i
                cols = slice(h * SIZE, (h + 1) * SIZE)
                value = acc[rows, cols] + dot(qs[last_bit, rows, cols], bkt[last_bit, cols, :])
                mean = jnp.mean(value * value, axis=-1, keepdims=True)
                ng[y, wave, rows, i * SIZE : (i + 1) * SIZE] = (value * lax.rsqrt(mean + 1e-05)).astype(BF16)
            own_normed(2 * wave + part, 0).start()
            own_normed(2 * wave + part, 1).start()

    def pass_normed(u):
        for side in range(2):
            own_normed(u, side).wait_recv()
            onward_normed(u, side).start()

    pass_normed(0)
    for c in over_x2:
        c.wait_recv()
    share.start()
    pass_normed(1)
    pass_normed(2)
    own_out.wait()
    share.wait_recv()

    def place(u):
        wave = u // 2
        return wave, slice(u % 2 * many, (u % 2 + 1) * many), slice(wave * 256, (wave + 1) * 256)

    for u in range(4):
        if u == 2:
            pass_normed(3)
        wave, rows, depth = place(u)
        product = dot(ng[y, wave, rows, :], wown[depth, :])
        product = product + dot(ng[left, wave, rows, :], wop[0, depth, :])
        product = product + dot(ng[right, wave, rows, :], wop[1, depth, :])
        pacc[wave, rows, :] = product
    for u in range(4):
        onward_normed(u, 0).wait_recv()
        onward_normed(u, 1).wait_recv()
        wave, rows, depth = place(u)
        product = pacc[wave, rows, :] + dot(ng[across, wave, rows, :], wop[2, depth, :])
        if wave == 0:
            pacc[0, rows, :] = product
        else:
            out_ref[rows, :] = (pacc[0, rows, :] + product).astype(BF16)

    for r in range(BLOCKS):
        for side in range(2):
            own_rows(r, side).wait_send()
            onward(r, side).wait_send()
            own_normed(r, side).wait_send()
            onward_normed(r, side).wait_send()
    for c in decay_copies + kv_fetch + kv_x + [kv_share] + kv_parts + fetch + over_z + over_x + over_x2 + [share]:
        c.wait_send()
    for wave in range(2):
        corner(wave, True).wait_send()
        corner(wave, False).wait_send()
        for bit in range(last_bit):
            if bit != 2:
                state_copy(bit, wave).wait_send()
            if bit > 0:
                hand_over(bit, wave).wait_send()

        @pl.when(is_source)
        def _(wave=wave):
            top_copy(wave, near, 0).wait_send()
            top_copy(wave, far, 1).wait_send()

        @pl.when(is_top)
        def _(wave=wave):
            hand_over(last_bit, wave).wait_send()


def body(tokens, log_decay, w_query, w_key, w_value, w_level, w_out):
    hbm = pl.BlockSpec(memory_space=pl.ANY)
    vmem = pl.BlockSpec(memory_space=pltpu.VMEM)
    dma = pltpu.SemaphoreType.DMA
    wide = HEADS * LEVELS
    return pl.pallas_call(
        kernel,
        name="layer",
        out_shape=pltpu.VMEM((ROWS, PART), BF16),
        in_specs=[hbm, vmem, hbm, hbm, hbm, vmem, hbm],
        out_specs=vmem,
        scratch_shapes=[
            pltpu.VMEM((4, ROWS, PART), BF16),
            pltpu.VMEM((4 * PART, HEADS * SIZE), BF16),
            pltpu.VMEM((4 * PART, 2 * SIZE), BF16),
            pltpu.VMEM((3, PART, 2 * SIZE), BF16),
            pltpu.VMEM((3, LATE, 2 * SIZE), BF16),
            pltpu.VMEM((3, LATE, 2 * SIZE), BF16),
            pltpu.VMEM((HEADS * SIZE, PART), BF16),
            pltpu.VMEM((3, HEADS * SIZE, PART), BF16),
            pltpu.VMEM((4, 2, ROWS, 2 * SIZE), BF16),
            pltpu.VMEM((2, ROWS, PART), F32),
            pltpu.VMEM((SIZE, ROWS), F32),
            pltpu.VMEM((ROWS, wide), F32),
            pltpu.VMEM((8, ROWS), F32),
            pltpu.VMEM((BLOCKS, 8, SIZE), F32),
            pltpu.VMEM((8, wide), F32),
            pltpu.VMEM((BITS - 1, 24, SIZE), F32),
            pltpu.VMEM((BITS - 1, 24, SIZE), F32),
            pltpu.VMEM((BITS - 1, 2, 8, SIZE), F32),
            pltpu.VMEM((2, 8, SIZE), F32),
            pltpu.VMEM((2, HEADS * SIZE, SIZE), BF16),
            pltpu.VMEM((ROWS, HEADS * SIZE), BF16),
            pltpu.VMEM((ROWS, SIZE), BF16),
            pltpu.VMEM((ROWS, SIZE), BF16),
            pltpu.VMEM((ROWS, HEADS * SIZE), F32),
            pltpu.VMEM((BITS, ROWS, HEADS * SIZE), BF16),
            pltpu.VMEM((BLOCKS, HEADS * SIZE, SIZE), F32),
            pltpu.VMEM((HEADS * SIZE, SIZE), BF16),
            pltpu.VMEM((HEADS * SIZE, SIZE), F32),
            pltpu.VMEM((BITS, HEADS * SIZE, SIZE), BF16),
            pltpu.VMEM((BITS, HEADS * SIZE, SIZE), BF16),
            dma((4 * BLOCKS,)), dma((4 * BLOCKS,)),
            dma((BITS - 1,)), dma((BITS - 1,)),
            dma((2 * BITS + 2,)), dma((2 * BITS,)),
            dma((2,)), dma((2,)),
            dma((2 * BITS,)), dma((2 * BITS,)),
            dma((12,)), dma((12,)),
            dma((10,)), dma((10,)),
            dma((4 * BLOCKS,)), dma((4 * BLOCKS,)),
            pltpu.SemaphoreType.REGULAR((2,)), dma((5,)),
        ],
        compiler_params=pltpu.CompilerParams(
            collective_id=0, has_side_effects=True, vmem_limit_bytes=56 << 20
        ),
        cost_estimate=pl.CostEstimate(flops=7_000_000_000, bytes_accessed=14_000_000, transcendentals=400_000),
    )(tokens, log_decay.T, w_query, w_key, w_value, w_level.T, w_out)


def solution(mesh):
    in_specs = (
        P("seq", "tp"),
        P("seq", "tp"),
        P(None, "tp"),
        P(None, "tp"),
        P(None, "tp"),
        P(None, "tp"),
        P("tp", None),
    )
    return jax.shard_map(
        body, mesh=mesh, in_specs=in_specs, out_specs=P("seq", "tp"), check_vma=False
    )
```

```python
import jax
import jax.numpy as jnp
from jax import lax
from jax.experimental import pallas as pl
from jax.experimental.pallas import tpu as pltpu
from jax.sharding import PartitionSpec as P

BLOCK = 128
F32 = jnp.float32
BF16 = jnp.bfloat16
MESH = pl.DeviceIdType.MESH
NEVER = -1e30
HEADS = 4
SIZE = 128
LEVELS = 9
ROWS = 512
BLOCKS = ROWS // BLOCK
PART = 1024
BITS = 6
EARLY = 2
LATE = ROWS - EARLY * BLOCK


def dot(a, b):
    return jnp.dot(a, b, preferred_element_type=F32)


def dot_t(a, b):
    return lax.dot_general(a, b, (((1,), (1,)), ((), ())), preferred_element_type=F32)


def split3(wide):
    high = wide.astype(BF16)
    rest = wide - high.astype(F32)
    middle = rest.astype(BF16)
    low = (rest - middle.astype(F32)).astype(BF16)
    return high, middle, low


def softplus(x):
    return jnp.maximum(x, 0.0) + jnp.log1p(jnp.exp(-jnp.abs(x)))


def kernel(
    x_ref, ld_ref, wq_ref, wk_ref, wv_ref, wl_ref, wo_ref, out_ref,
    xg, wq, wkv, wkp, psend, prec, wown, wop, ng, pacc,
    ldp, d36, dect, ends, offs, gsend, grecv, coef, pair, xin,
    qb, kb, vb, acc, qs, sb, sb16, run, ssend, bkt,
    tok_s, tok_r, dec_s, dec_r, st_s, st_r, xs, xr, fw_s, fw_r, wo_s, wo_r, kv_s, kv_r, nm_s, nm_r, ready, loc,
):
    y = lax.axis_index("tp")
    s = lax.axis_index("seq")
    core = lax.rem(s, 2)
    cx = lax.rem(lax.div(s, 2), 4)
    cz = lax.div(s, 8)
    right, left, across = lax.rem(y + 1, 4), lax.rem(y + 3, 4), lax.rem(y + 2, 4)
    to_right, to_left, to_across = {"tp": right}, {"tp": left}, {"tp": across}
    uppers = [core, lax.rem(cx, 2), lax.div(cx, 2), lax.rem(cz, 2), lax.rem(lax.div(cz, 2), 2), lax.div(cz, 4)]
    mates = [
        s + 1 - 2 * core,
        s + (1 - 2 * uppers[1]) * 2,
        s + (3 - 2 * cx) * 2,
        s + (1 - 2 * uppers[3]) * 8,
        s + (1 - 2 * uppers[4]) * 16,
    ]
    opposite = {"seq": s + (1 - 2 * uppers[5]) * 32}
    x_across = {"seq": s + (1 - 2 * uppers[2]) * 4}
    mates = [{"seq": m} for m in mates]
    is_top = cz >= 4
    is_source = jnp.logical_or(cz == 0, cz == 3)
    plane = lax.rem(s, 8)
    near = {"seq": jnp.where(cz == 0, 56, 32) + plane}
    far = {"seq": jnp.where(cz == 0, 48, 40) + plane}
    source = {"seq": jnp.where(cz < 6, 24, 0) + plane}

    def remote(src, dst, send, recv, device):
        return pltpu.make_async_remote_copy(
            src_ref=src, dst_ref=dst, send_sem=send, recv_sem=recv, device_id=device, device_id_type=MESH
        )

    locals_ = [
        pltpu.make_async_copy(x_ref, xg.at[y], loc.at[0]),
        pltpu.make_async_copy(wk_ref, wkv.at[:, pl.ds(0, SIZE)], loc.at[1]),
        pltpu.make_async_copy(wv_ref, wkv.at[:, pl.ds(SIZE, SIZE)], loc.at[2]),
        pltpu.make_async_copy(wq_ref, wq, loc.at[3]),
    ]
    own_out = pltpu.make_async_copy(wo_ref.at[:, pl.ds(pl.multiple_of(y * PART, PART), PART)], wown, loc.at[4])
    for c in locals_:
        c.start()

    @pl.when(jnp.logical_not(is_top))
    def _():
        bkt[BITS - 1] = jnp.zeros((HEADS * SIZE, SIZE), BF16)

    barrier = pltpu.get_barrier_semaphore()
    in_half = [to_right, to_left, to_across, x_across] + mates
    for peer in in_half:
        pl.semaphore_signal(barrier, inc=1, device_id=peer, device_id_type=MESH)

    @pl.when(jnp.logical_not(is_top))
    def _():
        pl.semaphore_signal(barrier, inc=1, device_id=opposite, device_id_type=MESH)

    @pl.when(is_source)
    def _():
        pl.semaphore_signal(barrier, inc=1, device_id=near, device_id_type=MESH)
        pl.semaphore_signal(barrier, inc=1, device_id=far, device_id_type=MESH)

    pl.semaphore_wait(barrier, len(in_half) + jnp.where(is_top, 2, 0))

    @pl.when(is_top)
    def _():
        pl.semaphore_signal(ready.at[0], inc=1, device_id=opposite, device_id_type=MESH)
        pl.semaphore_signal(ready.at[1], inc=1, device_id=source, device_id_type=MESH)

    wide_cols = pl.ds(pl.multiple_of(core * 512, 512), 512)
    cols_a = pl.ds(pl.multiple_of(core * 512, 256), 256)
    cols_b = pl.ds(pl.multiple_of(core * 512 + 256, 256), 256)
    piece = cx * 8 + cz

    def some_rows(start, count):
        return pl.ds(pl.multiple_of(start * 16, 16), count * 16)

    def spread_copy(i, rows, cols, device):
        part = wop.at[:, rows, cols]
        return remote(part, part, wo_s.at[i], wo_r.at[i], device)

    fetch = []
    for i, (peer, device) in enumerate(((right, to_right), (left, to_left), (across, to_across))):
        there = pl.ds(pl.multiple_of(peer * PART + core * 512, 512), 512)
        rows = some_rows(piece, 1)
        fetch.append(remote(wo_ref.at[rows, there], wop.at[i, rows, wide_cols], wo_s.at[i], wo_r.at[i], device))
    over_z = [
        spread_copy(3, some_rows(piece, 1), wide_cols, mates[3]),
        spread_copy(4, some_rows(piece - lax.rem(cz, 2), 2), wide_cols, mates[4]),
        spread_copy(5, some_rows(piece - lax.rem(cz, 4), 4), wide_cols, opposite),
    ]
    over_x = [
        spread_copy(6, some_rows(cx * 8, 8), cols_a, mates[1]),
        spread_copy(7, some_rows(cx * 8, 8), cols_b, mates[2]),
    ]
    over_x2 = [
        spread_copy(8, some_rows(lax.div(cx, 2) * 16, 16), cols_a, mates[2]),
        spread_copy(9, some_rows(cx * 8, 8), cols_b, mates[1]),
        spread_copy(10, some_rows((3 - cx) * 8, 8), cols_b, mates[1]),
    ]
    share = spread_copy(11, pl.ds(0, ROWS), wide_cols, mates[0])

    eighth = pl.ds(pl.multiple_of((core * 4 + cx) * 128, 128), 128)
    core_rows = pl.ds(pl.multiple_of(core * 512, 512), 512)
    kv_fetch = []
    for i, (peer, device) in enumerate(((right, to_right), (left, to_left), (across, to_across))):
        there = pl.ds(pl.multiple_of(peer * PART + (core * 4 + cx) * 128, 128), 128)
        kv_fetch.append(remote(wkv.at[there], wkp.at[i, eighth], kv_s.at[i], kv_r.at[i], device))
    kv_x = [
        remote(wkp.at[:, eighth], wkp.at[:, eighth], kv_s.at[3 + i], kv_r.at[3 + i], device)
        for i, device in enumerate((mates[1], mates[2], x_across))
    ]
    kv_share = remote(wkp.at[:, core_rows], wkp.at[:, core_rows], kv_s.at[6], kv_r.at[6], mates[0])
    kv_parts = [
        remote(psend.at[0], prec.at[1], kv_s.at[7], kv_r.at[7], to_left),
        remote(psend.at[1], prec.at[0], kv_s.at[8], kv_r.at[8], to_right),
        remote(psend.at[2], prec.at[2], kv_s.at[9], kv_r.at[9], to_across),
    ]
    locals_[1].wait()
    locals_[2].wait()
    for c in kv_fetch:
        c.start()

    half = BLOCK // 2

    def own_rows(r, side):
        rows = pl.ds(r * BLOCK, BLOCK)
        i = 2 * r + side
        return remote(x_ref.at[rows], xg.at[y, rows], tok_s.at[i], tok_r.at[i], to_left if side else to_right)

    def onward(r, side):
        rows = pl.ds(r * BLOCK + side * half, half)
        i = 2 * BLOCKS + 2 * r + side
        owner = right if side else left
        return remote(xg.at[owner, rows], xg.at[owner, rows], tok_s.at[i], tok_r.at[i], to_left if side else to_right)

    def send_own(r):
        own_rows(r, 0).start()
        own_rows(r, 1).start()

    def pass_on(r):
        for side in range(2):
            own_rows(r, side).wait_recv()
            onward(r, side).start()

    ldp[...] = jnp.zeros_like(ldp)
    ldp[0:HEADS, :] = ld_ref[...]
    row = lax.broadcasted_iota(jnp.int32, (ROWS, ROWS), 0)
    col = lax.broadcasted_iota(jnp.int32, (ROWS, ROWS), 1)
    lower = (row >= col).astype(F32).astype(BF16)
    upper_tri = (row <= col).astype(F32).astype(BF16)
    wide_row = lax.broadcasted_iota(jnp.int32, (BLOCK, HEADS * LEVELS), 0)
    wide_col = lax.broadcasted_iota(jnp.int32, (BLOCK, HEADS * LEVELS), 1)
    spread = (lax.div(wide_col, LEVELS) == wide_row).astype(F32).astype(BF16)
    level_of = lax.rem(lax.broadcasted_iota(jnp.int32, (8, HEADS * LEVELS), 1), LEVELS)
    spread_decay = sum(dot(lower, dot(p, spread).astype(BF16)) for p in split3(jnp.transpose(ldp[...])))
    d36[...] = spread_decay
    along = sum(dot(p, upper_tri) for p in split3(ldp[0:16, :]))
    dect[...] = along[0:8]
    for c in range(BLOCKS):
        last = (c + 1) * BLOCK - 1
        ends[c] = jnp.broadcast_to(dect[:, last : last + 1], (8, SIZE))
    gsend[0] = jnp.zeros((24, SIZE), F32)
    gsend[0, 0:8] = ends[BLOCKS - 1]
    gsend[0, 8:16, 0 : HEADS * LEVELS] = jnp.broadcast_to(d36[ROWS - 1 : ROWS, :], (8, HEADS * LEVELS))
    before = jnp.zeros((8, HEADS * LEVELS), F32)
    gap_off = jnp.zeros((8, HEADS * LEVELS), F32)
    decay_copies = []
    for bit in range(BITS - 1):
        up = uppers[bit].astype(F32)
        c = remote(gsend.at[bit], grecv.at[bit], dec_s.at[bit], dec_r.at[bit], mates[bit])
        c.start()
        if bit == 0:
            send_own(0)
            for d in fetch:
                d.start()
        if bit == 2:
            send_own(1)
            for d in kv_fetch:
                d.wait_recv()
            for d in kv_x:
                d.start()
            for d in fetch:
                d.wait_recv()
            over_z[0].start()
        if bit == 3:
            pass_on(0)
        if bit == 4:
            over_z[0].wait_recv()
            over_z[1].start()
            pass_on(1)
            for d in kv_x:
                d.wait_recv()
            kv_share.start()
        c.wait_recv()
        decay_copies.append(c)
        mine = gsend[bit]
        other = grecv[bit]
        coef[bit, 0] = up + (1.0 - up) * jnp.exp(other[0:8])
        coef[bit, 1] = up * jnp.exp(mine[0:8]) + (1.0 - up)
        gap_off = gap_off + jnp.where(level_of == 3 + bit, up * before + (1.0 - up) * NEVER, 0.0)
        before = before + up * other[8:16, 0 : HEADS * LEVELS]
        if bit < BITS - 2:
            gsend[bit + 1, 0:16] = mine[0:16] + other[0:16]
            gsend[bit + 1, 16:24] = mine[0:8]
        if bit == 2:
            third = other[16:24]
            fourth = other[0:8] - third
            side = uppers[1].astype(F32)
            pair[0] = side * jnp.exp(fourth) + (1.0 - side)
            pair[1] = side + (1.0 - side) * jnp.exp(third)
    up = uppers[BITS - 1].astype(F32)
    gap_off = gap_off + jnp.where(level_of == 3 + BITS - 1, up * before + (1.0 - up) * NEVER, 0.0)
    offs[...] = gap_off
    for c in (locals_[0], locals_[3]):
        c.wait()

    owners = (y, left, right, across)

    def project(r, weights, who=owners):
        rows = pl.ds(r * BLOCK, BLOCK)
        return sum(dot(xg[i, rows, :], weights[pl.ds(pl.multiple_of(i * PART, PART), PART), :]) for i in who)

    def keys_part(r):
        rows = pl.ds(r * BLOCK, BLOCK)
        part = project(r, wkv, owners[:3])
        onward(r, 0).wait_recv()
        onward(r, 1).wait_recv()
        finish_keys(r, part + project(r, wkv, owners[3:]))

    def keys_late(r):
        rows = pl.ds((r - EARLY) * BLOCK, BLOCK)
        both = project(r, wkv, owners[:1])
        for i in range(3):
            both = both + prec[i, rows, :].astype(F32)
        finish_keys(r, both)

    def finish_keys(r, both):
        rows = pl.ds(r * BLOCK, BLOCK)
        values = both[:, SIZE:].astype(BF16)
        kb[rows, :] = both[:, :SIZE].astype(BF16)
        vb[rows, :] = values
        k_t = jnp.transpose(both[:, :SIZE].astype(BF16).astype(F32))
        weight = jnp.exp(ends[r] - dect[:, r * BLOCK : (r + 1) * BLOCK])
        for h in range(HEADS):
            scaled = (k_t * weight[h : h + 1, :]).astype(BF16)
            sb[r, h * SIZE : (h + 1) * SIZE, :] = dot(scaled, values)

    def fade_of(c, before_c, h):
        return jnp.exp(ends[c] - ends[before_c])[h : h + 1, :]

    def query_part(r):
        rows = slice(r * BLOCK, (r + 1) * BLOCK)
        qb[rows, :] = project(r, wq).astype(BF16)
        weight = softplus(sum(dot_t(xg[i, rows, :], wl_ref[:, i * PART : (i + 1) * PART]) for i in range(4)))
        kind = level_of[0:1]
        off = offs[0:1, :]
        off = jnp.where(kind == 1, -d36[r * BLOCK - 1 : r * BLOCK, :] if r % 2 else NEVER, off)
        off = jnp.where(kind == 2, -d36[2 * BLOCK - 1 : 2 * BLOCK, :] if r >= 2 else NEVER, off)
        here = d36[rows, :]
        power = jnp.where(kind == 0, 0.0, here + off)
        factor = weight * jnp.exp(power)
        keys = kb[rows, :]
        values = vb[rows, :]
        inside_row = lax.broadcasted_iota(jnp.int32, (BLOCK, BLOCK), 0)
        inside_col = lax.broadcasted_iota(jnp.int32, (BLOCK, BLOCK), 1)
        causal = inside_row >= inside_col
        along_here = dect[:, rows]
        for h in range(HEADS):
            cols = slice(h * SIZE, (h + 1) * SIZE)
            query = qb[rows, cols]
            wide = query.astype(F32)
            scores = dot_t(query, keys)
            gap = here[:, h * LEVELS : h * LEVELS + 1] - along_here[h : h + 1, :]
            mixing = jnp.exp(jnp.where(causal, gap, NEVER)) * scores * factor[:, h * LEVELS : h * LEVELS + 1]
            total = dot(mixing.astype(BF16), values)
            if r % 2:
                near_query = (wide * factor[:, h * LEVELS + 1 : h * LEVELS + 2]).astype(BF16)
                total = total + dot(near_query, sb[r - 1, cols, :].astype(BF16))
            if r >= 2:
                late_query = (wide * factor[:, h * LEVELS + 2 : h * LEVELS + 3]).astype(BF16)
                total = total + dot(late_query, sb16[cols, :])
            acc[rows, cols] = total
            for bit in range(BITS):
                at = h * LEVELS + 3 + bit
                qs[bit, rows, cols] = (wide * factor[:, at : at + 1]).astype(BF16)

    def pair_sum():
        for h in range(HEADS):
            cols = slice(h * SIZE, (h + 1) * SIZE)
            sb16[cols, :] = (sb[1, cols, :] + fade_of(1, 0, h) * sb[0, cols, :]).astype(BF16)

    keys_part(0)
    kv_share.wait_recv()
    for i in (2, 0, 1):
        psend[i] = dot(xg[y, EARLY * BLOCK :, :], wkp[i]).astype(BF16)
        kv_parts[i].start()
    over_z[1].wait_recv()

    @pl.when(jnp.logical_not(is_top))
    def _():
        pl.semaphore_wait(ready.at[0], 1)

    over_z[2].start()
    keys_part(1)
    pair_sum()
    query_part(0)
    query_part(1)
    send_own(2)
    for c in kv_parts:
        c.wait_recv()
    send_own(3)
    for r in range(EARLY, BLOCKS):
        keys_late(r)
    for h in range(HEADS):
        cols = slice(h * SIZE, (h + 1) * SIZE)
        first = sb[1, cols, :] + fade_of(1, 0, h) * sb[0, cols, :]
        second = sb[3, cols, :] + fade_of(3, 2, h) * sb[2, cols, :]
        whole = second + fade_of(3, 1, h) * first
        run[cols, :] = whole
        ssend[0, cols, :] = whole.astype(BF16)

    last_bit = BITS - 1

    def head_rows(wave):
        return pl.ds(pl.multiple_of((2 * wave + core) * SIZE, SIZE), SIZE)

    def state_copy(bit, wave):
        rows = pl.ds(2 * wave * SIZE, 2 * SIZE) if bit == 0 else head_rows(wave)
        i = 2 * bit + wave
        return remote(ssend.at[bit, rows], bkt.at[bit, rows], st_s.at[i], st_r.at[i], mates[bit])

    def top_copy(wave, device, place):
        rows = head_rows(wave)
        i = 2 * last_bit + wave
        return remote(ssend.at[last_bit, rows], bkt.at[last_bit, rows], st_s.at[i + 2 * place], st_r.at[i], device)

    def hand_over(bit, wave):
        rows = head_rows(wave)
        i = 2 * bit + wave
        return remote(bkt.at[bit, rows], bkt.at[bit, rows], fw_s.at[i], fw_r.at[i], mates[0])

    for wave in range(2):
        state_copy(0, wave).start()
    own_out.start()

    def take(bit):
        for h in range(HEADS):
            cols = slice(h * SIZE, (h + 1) * SIZE)
            acc[:, cols] += dot(qs[bit, :, cols], bkt[bit, cols, :])

    def corner(wave, third):
        rows = head_rows(wave)
        if third:
            return remote(ssend.at[1, rows], xin.at[0, rows], st_s.at[4 + wave], st_r.at[4 + wave], mates[2])
        return remote(ssend.at[1, rows], xin.at[1, rows], xs.at[wave], xr.at[wave], x_across)

    def scale(row, wave):
        return row[pl.ds(2 * wave + core, 1), :]

    def merge(bit, wave, other):
        one = head_rows(wave)
        return scale(coef.at[bit, 0], wave) * run[one, :] + scale(coef.at[bit, 1], wave) * other

    for wave in range(2):
        one = head_rows(wave)
        state_copy(0, wave).wait_recv()
        merged = merge(0, wave, bkt[0, one, :].astype(F32))
        run[one, :] = merged
        ssend[1, one, :] = merged.astype(BF16)
        corner(wave, False).start()
        state_copy(1, wave).start()
        corner(wave, True).start()
    for wave in range(2):
        one = head_rows(wave)
        state_copy(1, wave).wait_recv()
        corner(wave, True).wait_recv()
        corner(wave, False).wait_recv()
        run[one, :] = merge(1, wave, bkt[1, one, :].astype(F32))
        second = scale(pair.at[0], wave) * xin[0, one, :].astype(F32) + scale(pair.at[1], wave) * xin[1, one, :].astype(F32)
        merged = merge(2, wave, second)
        run[one, :] = merged
        ssend[3, one, :] = merged.astype(BF16)
        state_copy(3, wave).start()
        bkt[2, one, :] = second.astype(BF16)
        hand_over(1, wave).start()
        hand_over(2, wave).start()
    over_z[2].wait_recv()
    for c in over_x:
        c.start()
    pass_on(2)
    for wave in range(2):
        one = head_rows(wave)
        state_copy(3, wave).wait_recv()
        merged = merge(3, wave, bkt[3, one, :].astype(F32))
        run[one, :] = merged
        ssend[4, one, :] = merged.astype(BF16)
        state_copy(4, wave).start()
        hand_over(3, wave).start()
    pass_on(3)
    for wave in range(2):
        one = head_rows(wave)
        state_copy(4, wave).wait_recv()
        ssend[last_bit, one, :] = merge(4, wave, bkt[4, one, :].astype(F32)).astype(BF16)

        @pl.when(is_source)
        def _(wave=wave):
            if wave == 0:
                pl.semaphore_wait(ready.at[1], 2)
            top_copy(wave, near, 0).start()
            top_copy(wave, far, 1).start()

        hand_over(4, wave).start()
    for c in over_x:
        c.wait_recv()
    for c in over_x2:
        c.start()
    for r in range(2, BLOCKS):
        onward(r, 0).wait_recv()
        onward(r, 1).wait_recv()
        query_part(r)

    many = ROWS // 2

    def own_normed(u, side):
        part = ng.at[y, u // 2, pl.ds(u % 2 * many, many)]
        i = 2 * u + side
        return remote(part, part, nm_s.at[i], nm_r.at[i], to_left if side else to_right)

    def onward_normed(u, side):
        part = ng.at[right if side else left, u // 2, pl.ds(u % 2 * many + side * BLOCK, BLOCK)]
        i = 8 + 2 * u + side
        return remote(part, part, nm_s.at[i], nm_r.at[i], to_left if side else to_right)

    for wave in range(2):

        @pl.when(is_top)
        def _(wave=wave):
            top_copy(wave, source, 0).wait_recv()
            hand_over(last_bit, wave).start()

    for bit in range(last_bit):
        if bit > 0:
            for wave in range(2):
                hand_over(bit, wave).wait_recv()
        take(bit)
    for wave in range(2):

        @pl.when(is_top)
        def _(wave=wave):
            hand_over(last_bit, wave).wait_recv()

        for part in range(2):
            rows = slice(part * many, (part + 1) * many)
            for i in range(2):
                h = 2 * wave + i
                cols = slice(h * SIZE, (h + 1) * SIZE)
                value = acc[rows, cols] + dot(qs[last_bit, rows, cols], bkt[last_bit, cols, :])
                mean = jnp.mean(value * value, axis=-1, keepdims=True)
                ng[y, wave, rows, i * SIZE : (i + 1) * SIZE] = (value * lax.rsqrt(mean + 1e-05)).astype(BF16)
            own_normed(2 * wave + part, 0).start()
            own_normed(2 * wave + part, 1).start()

    def pass_normed(u):
        for side in range(2):
            own_normed(u, side).wait_recv()
            onward_normed(u, side).start()

    pass_normed(0)
    for c in over_x2:
        c.wait_recv()
    share.start()
    pass_normed(1)
    pass_normed(2)
    own_out.wait()
    share.wait_recv()

    def place(u):
        wave = u // 2
        return wave, slice(u % 2 * many, (u % 2 + 1) * many), slice(wave * 256, (wave + 1) * 256)

    for u in range(4):
        if u == 2:
            pass_normed(3)
        wave, rows, depth = place(u)
        product = dot(ng[y, wave, rows, :], wown[depth, :])
        product = product + dot(ng[left, wave, rows, :], wop[0, depth, :])
        product = product + dot(ng[right, wave, rows, :], wop[1, depth, :])
        pacc[wave, rows, :] = product
    for u in range(4):
        onward_normed(u, 0).wait_recv()
        onward_normed(u, 1).wait_recv()
        wave, rows, depth = place(u)
        product = pacc[wave, rows, :] + dot(ng[across, wave, rows, :], wop[2, depth, :])
        if wave == 0:
            pacc[0, rows, :] = product
        else:
            out_ref[rows, :] = (pacc[0, rows, :] + product).astype(BF16)

    for r in range(BLOCKS):
        for side in range(2):
            own_rows(r, side).wait_send()
            onward(r, side).wait_send()
            own_normed(r, side).wait_send()
            onward_normed(r, side).wait_send()
    for c in decay_copies + kv_fetch + kv_x + [kv_share] + kv_parts + fetch + over_z + over_x + over_x2 + [share]:
        c.wait_send()
    for wave in range(2):
        corner(wave, True).wait_send()
        corner(wave, False).wait_send()
        for bit in range(last_bit):
            if bit != 2:
                state_copy(bit, wave).wait_send()
            if bit > 0:
                hand_over(bit, wave).wait_send()

        @pl.when(is_source)
        def _(wave=wave):
            top_copy(wave, near, 0).wait_send()
            top_copy(wave, far, 1).wait_send()

        @pl.when(is_top)
        def _(wave=wave):
            hand_over(last_bit, wave).wait_send()


def body(tokens, log_decay, w_query, w_key, w_value, w_level, w_out):
    hbm = pl.BlockSpec(memory_space=pl.ANY)
    vmem = pl.BlockSpec(memory_space=pltpu.VMEM)
    dma = pltpu.SemaphoreType.DMA
    wide = HEADS * LEVELS
    return pl.pallas_call(
        kernel,
        name="layer",
        out_shape=pltpu.VMEM((ROWS, PART), BF16),
        in_specs=[hbm, vmem, hbm, hbm, hbm, vmem, hbm],
        out_specs=vmem,
        scratch_shapes=[
            pltpu.VMEM((4, ROWS, PART), BF16),
            pltpu.VMEM((4 * PART, HEADS * SIZE), BF16),
            pltpu.VMEM((4 * PART, 2 * SIZE), BF16),
            pltpu.VMEM((3, PART, 2 * SIZE), BF16),
            pltpu.VMEM((3, LATE, 2 * SIZE), BF16),
            pltpu.VMEM((3, LATE, 2 * SIZE), BF16),
            pltpu.VMEM((HEADS * SIZE, PART), BF16),
            pltpu.VMEM((3, HEADS * SIZE, PART), BF16),
            pltpu.VMEM((4, 2, ROWS, 2 * SIZE), BF16),
            pltpu.VMEM((2, ROWS, PART), F32),
            pltpu.VMEM((SIZE, ROWS), F32),
            pltpu.VMEM((ROWS, wide), F32),
            pltpu.VMEM((8, ROWS), F32),
            pltpu.VMEM((BLOCKS, 8, SIZE), F32),
            pltpu.VMEM((8, wide), F32),
            pltpu.VMEM((BITS - 1, 24, SIZE), F32),
            pltpu.VMEM((BITS - 1, 24, SIZE), F32),
            pltpu.VMEM((BITS - 1, 2, 8, SIZE), F32),
            pltpu.VMEM((2, 8, SIZE), F32),
            pltpu.VMEM((2, HEADS * SIZE, SIZE), BF16),
            pltpu.VMEM((ROWS, HEADS * SIZE), BF16),
            pltpu.VMEM((ROWS, SIZE), BF16),
            pltpu.VMEM((ROWS, SIZE), BF16),
            pltpu.VMEM((ROWS, HEADS * SIZE), F32),
            pltpu.VMEM((BITS, ROWS, HEADS * SIZE), BF16),
            pltpu.VMEM((BLOCKS, HEADS * SIZE, SIZE), F32),
            pltpu.VMEM((HEADS * SIZE, SIZE), BF16),
            pltpu.VMEM((HEADS * SIZE, SIZE), F32),
            pltpu.VMEM((BITS, HEADS * SIZE, SIZE), BF16),
            pltpu.VMEM((BITS, HEADS * SIZE, SIZE), BF16),
            dma((4 * BLOCKS,)), dma((4 * BLOCKS,)),
            dma((BITS - 1,)), dma((BITS - 1,)),
            dma((2 * BITS + 2,)), dma((2 * BITS,)),
            dma((2,)), dma((2,)),
            dma((2 * BITS,)), dma((2 * BITS,)),
            dma((12,)), dma((12,)),
            dma((10,)), dma((10,)),
            dma((4 * BLOCKS,)), dma((4 * BLOCKS,)),
            pltpu.SemaphoreType.REGULAR((2,)), dma((5,)),
        ],
        compiler_params=pltpu.CompilerParams(
            collective_id=0, has_side_effects=True, vmem_limit_bytes=56 << 20
        ),
        cost_estimate=pl.CostEstimate(flops=7_000_000_000, bytes_accessed=14_000_000, transcendentals=400_000),
    )(tokens, log_decay.T, w_query, w_key, w_value, w_level.T, w_out)


def solution(mesh):
    in_specs = (
        P("seq", "tp"),
        P("seq", "tp"),
        P(None, "tp"),
        P(None, "tp"),
        P(None, "tp"),
        P(None, "tp"),
        P("tp", None),
    )
    return jax.shard_map(
        body, mesh=mesh, in_specs=in_specs, out_specs=P("seq", "tp"), check_vma=False
    )
```

```python
import jax
import jax.numpy as jnp
from jax import lax
from jax.experimental import pallas as pl
from jax.experimental.pallas import tpu as pltpu
from jax.sharding import PartitionSpec as P

BLOCK = 128
F32 = jnp.float32
BF16 = jnp.bfloat16
MESH = pl.DeviceIdType.MESH
NEVER = -1e30
HEADS = 4
SIZE = 128
LEVELS = 9
ROWS = 512
BLOCKS = ROWS // BLOCK
PART = 1024
BITS = 6
EARLY = 2
LATE = ROWS - EARLY * BLOCK


def dot(a, b):
    return jnp.dot(a, b, preferred_element_type=F32)


def dot_t(a, b):
    return lax.dot_general(a, b, (((1,), (1,)), ((), ())), preferred_element_type=F32)


def split3(wide):
    high = wide.astype(BF16)
    rest = wide - high.astype(F32)
    middle = rest.astype(BF16)
    low = (rest - middle.astype(F32)).astype(BF16)
    return high, middle, low


def softplus(x):
    return jnp.maximum(x, 0.0) + jnp.log1p(jnp.exp(-jnp.abs(x)))


def kernel(
    x_ref, ld_ref, wq_ref, wk_ref, wv_ref, wl_ref, wo_ref, out_ref,
    xg, wq, wkv, wkp, psend, prec, wown, wop, ng, pacc,
    ldp, d36, dect, ends, offs, gsend, grecv, coef, pair, xin,
    qb, kb, vb, acc, qs, sb, sb16, run, ssend, bkt,
    tok_s, tok_r, dec_s, dec_r, st_s, st_r, xs, xr, fw_s, fw_r, wo_s, wo_r, kv_s, kv_r, nm_s, nm_r, ready, loc,
):
    y = lax.axis_index("tp")
    s = lax.axis_index("seq")
    core = lax.rem(s, 2)
    cx = lax.rem(lax.div(s, 2), 4)
    cz = lax.div(s, 8)
    right, left, across = lax.rem(y + 1, 4), lax.rem(y + 3, 4), lax.rem(y + 2, 4)
    to_right, to_left, to_across = {"tp": right}, {"tp": left}, {"tp": across}
    uppers = [core, lax.rem(cx, 2), lax.div(cx, 2), lax.rem(cz, 2), lax.rem(lax.div(cz, 2), 2), lax.div(cz, 4)]
    mates = [
        s + 1 - 2 * core,
        s + (1 - 2 * uppers[1]) * 2,
        s + (3 - 2 * cx) * 2,
        s + (1 - 2 * uppers[3]) * 8,
        s + (1 - 2 * uppers[4]) * 16,
    ]
    opposite = {"seq": s + (1 - 2 * uppers[5]) * 32}
    x_across = {"seq": s + (1 - 2 * uppers[2]) * 4}
    mates = [{"seq": m} for m in mates]
    is_top = cz >= 4
    is_source = jnp.logical_or(cz == 0, cz == 3)
    plane = lax.rem(s, 8)
    near = {"seq": jnp.where(cz == 0, 56, 32) + plane}
    far = {"seq": jnp.where(cz == 0, 48, 40) + plane}
    source = {"seq": jnp.where(cz < 6, 24, 0) + plane}

    def remote(src, dst, send, recv, device):
        return pltpu.make_async_remote_copy(
            src_ref=src, dst_ref=dst, send_sem=send, recv_sem=recv, device_id=device, device_id_type=MESH
        )

    locals_ = [
        pltpu.make_async_copy(x_ref, xg.at[y], loc.at[0]),
        pltpu.make_async_copy(wk_ref, wkv.at[:, pl.ds(0, SIZE)], loc.at[1]),
        pltpu.make_async_copy(wv_ref, wkv.at[:, pl.ds(SIZE, SIZE)], loc.at[2]),
        pltpu.make_async_copy(wq_ref, wq, loc.at[3]),
    ]
    own_out = pltpu.make_async_copy(wo_ref.at[:, pl.ds(pl.multiple_of(y * PART, PART), PART)], wown, loc.at[4])
    for c in locals_:
        c.start()

    @pl.when(jnp.logical_not(is_top))
    def _():
        bkt[BITS - 1] = jnp.zeros((HEADS * SIZE, SIZE), BF16)

    barrier = pltpu.get_barrier_semaphore()
    in_half = [to_right, to_left, to_across, x_across] + mates
    for peer in in_half:
        pl.semaphore_signal(barrier, inc=1, device_id=peer, device_id_type=MESH)

    @pl.when(jnp.logical_not(is_top))
    def _():
        pl.semaphore_signal(barrier, inc=1, device_id=opposite, device_id_type=MESH)

    @pl.when(is_source)
    def _():
        pl.semaphore_signal(barrier, inc=1, device_id=near, device_id_type=MESH)
        pl.semaphore_signal(barrier, inc=1, device_id=far, device_id_type=MESH)

    pl.semaphore_wait(barrier, len(in_half) + jnp.where(is_top, 2, 0))

    @pl.when(is_top)
    def _():
        pl.semaphore_signal(ready.at[0], inc=1, device_id=opposite, device_id_type=MESH)
        pl.semaphore_signal(ready.at[1], inc=1, device_id=source, device_id_type=MESH)

    wide_cols = pl.ds(pl.multiple_of(core * 512, 512), 512)
    cols_a = pl.ds(pl.multiple_of(core * 512, 256), 256)
    cols_b = pl.ds(pl.multiple_of(core * 512 + 256, 256), 256)
    piece = cx * 8 + cz

    def some_rows(start, count):
        return pl.ds(pl.multiple_of(start * 16, 16), count * 16)

    def spread_copy(i, rows, cols, device):
        part = wop.at[:, rows, cols]
        return remote(part, part, wo_s.at[i], wo_r.at[i], device)

    fetch = []
    for i, (peer, device) in enumerate(((right, to_right), (left, to_left), (across, to_across))):
        there = pl.ds(pl.multiple_of(peer * PART + core * 512, 512), 512)
        rows = some_rows(piece, 1)
        fetch.append(remote(wo_ref.at[rows, there], wop.at[i, rows, wide_cols], wo_s.at[i], wo_r.at[i], device))
    over_z = [
        spread_copy(3, some_rows(piece, 1), wide_cols, mates[3]),
        spread_copy(4, some_rows(piece - lax.rem(cz, 2), 2), wide_cols, mates[4]),
        spread_copy(5, some_rows(piece - lax.rem(cz, 4), 4), wide_cols, opposite),
    ]
    over_x = [
        spread_copy(6, some_rows(cx * 8, 8), cols_a, mates[1]),
        spread_copy(7, some_rows(cx * 8, 8), cols_b, mates[2]),
    ]
    over_x2 = [
        spread_copy(8, some_rows(lax.div(cx, 2) * 16, 16), cols_a, mates[2]),
        spread_copy(9, some_rows(cx * 8, 8), cols_b, mates[1]),
        spread_copy(10, some_rows((3 - cx) * 8, 8), cols_b, mates[1]),
    ]
    share = spread_copy(11, pl.ds(0, ROWS), wide_cols, mates[0])

    eighth = pl.ds(pl.multiple_of((core * 4 + cx) * 128, 128), 128)
    core_rows = pl.ds(pl.multiple_of(core * 512, 512), 512)
    kv_fetch = []
    for i, (peer, device) in enumerate(((right, to_right), (left, to_left), (across, to_across))):
        there = pl.ds(pl.multiple_of(peer * PART + (core * 4 + cx) * 128, 128), 128)
        kv_fetch.append(remote(wkv.at[there], wkp.at[i, eighth], kv_s.at[i], kv_r.at[i], device))
    kv_x = [
        remote(wkp.at[:, eighth], wkp.at[:, eighth], kv_s.at[3 + i], kv_r.at[3 + i], device)
        for i, device in enumerate((mates[1], mates[2], x_across))
    ]
    kv_share = remote(wkp.at[:, core_rows], wkp.at[:, core_rows], kv_s.at[6], kv_r.at[6], mates[0])
    kv_parts = [
        remote(psend.at[0], prec.at[1], kv_s.at[7], kv_r.at[7], to_left),
        remote(psend.at[1], prec.at[0], kv_s.at[8], kv_r.at[8], to_right),
        remote(psend.at[2], prec.at[2], kv_s.at[9], kv_r.at[9], to_across),
    ]
    locals_[1].wait()
    locals_[2].wait()
    for c in kv_fetch:
        c.start()

    half = BLOCK // 2

    def own_rows(r, side):
        rows = pl.ds(r * BLOCK, BLOCK)
        i = 2 * r + side
        return remote(x_ref.at[rows], xg.at[y, rows], tok_s.at[i], tok_r.at[i], to_left if side else to_right)

    def onward(r, side):
        rows = pl.ds(r * BLOCK + side * half, half)
        i = 2 * BLOCKS + 2 * r + side
        owner = right if side else left
        return remote(xg.at[owner, rows], xg.at[owner, rows], tok_s.at[i], tok_r.at[i], to_left if side else to_right)

    def send_own(r):
        own_rows(r, 0).start()
        own_rows(r, 1).start()

    def pass_on(r):
        for side in range(2):
            own_rows(r, side).wait_recv()
            onward(r, side).start()

    ldp[...] = jnp.zeros_like(ldp)
    ldp[0:HEADS, :] = ld_ref[...]
    row = lax.broadcasted_iota(jnp.int32, (ROWS, ROWS), 0)
    col = lax.broadcasted_iota(jnp.int32, (ROWS, ROWS), 1)
    lower = (row >= col).astype(F32).astype(BF16)
    upper_tri = (row <= col).astype(F32).astype(BF16)
    wide_row = lax.broadcasted_iota(jnp.int32, (BLOCK, HEADS * LEVELS), 0)
    wide_col = lax.broadcasted_iota(jnp.int32, (BLOCK, HEADS * LEVELS), 1)
    spread = (lax.div(wide_col, LEVELS) == wide_row).astype(F32).astype(BF16)
    level_of = lax.rem(lax.broadcasted_iota(jnp.int32, (8, HEADS * LEVELS), 1), LEVELS)
    spread_decay = sum(dot(lower, dot(p, spread).astype(BF16)) for p in split3(jnp.transpose(ldp[...])))
    d36[...] = spread_decay
    along = sum(dot(p, upper_tri) for p in split3(ldp[0:16, :]))
    dect[...] = along[0:8]
    for c in range(BLOCKS):
        last = (c + 1) * BLOCK - 1
        ends[c] = jnp.broadcast_to(dect[:, last : last + 1], (8, SIZE))
    gsend[0] = jnp.zeros((24, SIZE), F32)
    gsend[0, 0:8] = ends[BLOCKS - 1]
    gsend[0, 8:16, 0 : HEADS * LEVELS] = jnp.broadcast_to(d36[ROWS - 1 : ROWS, :], (8, HEADS * LEVELS))
    before = jnp.zeros((8, HEADS * LEVELS), F32)
    gap_off = jnp.zeros((8, HEADS * LEVELS), F32)
    decay_copies = []
    for bit in range(BITS - 1):
        up = uppers[bit].astype(F32)
        c = remote(gsend.at[bit], grecv.at[bit], dec_s.at[bit], dec_r.at[bit], mates[bit])
        c.start()
        if bit == 0:
            send_own(0)
            for d in fetch:
                d.start()
        if bit == 1:
            send_own(1)
        if bit == 2:
            for d in kv_fetch:
                d.wait_recv()
            for d in kv_x:
                d.start()
            for d in fetch:
                d.wait_recv()
            over_z[0].start()
        if bit == 3:
            pass_on(0)
        if bit == 4:
            over_z[0].wait_recv()
            over_z[1].start()
            pass_on(1)
            for d in kv_x:
                d.wait_recv()
            kv_share.start()
        c.wait_recv()
        decay_copies.append(c)
        mine = gsend[bit]
        other = grecv[bit]
        coef[bit, 0] = up + (1.0 - up) * jnp.exp(other[0:8])
        coef[bit, 1] = up * jnp.exp(mine[0:8]) + (1.0 - up)
        gap_off = gap_off + jnp.where(level_of == 3 + bit, up * before + (1.0 - up) * NEVER, 0.0)
        before = before + up * other[8:16, 0 : HEADS * LEVELS]
        if bit < BITS - 2:
            gsend[bit + 1, 0:16] = mine[0:16] + other[0:16]
            gsend[bit + 1, 16:24] = mine[0:8]
        if bit == 2:
            third = other[16:24]
            fourth = other[0:8] - third
            side = uppers[1].astype(F32)
            pair[0] = side * jnp.exp(fourth) + (1.0 - side)
            pair[1] = side + (1.0 - side) * jnp.exp(third)
    up = uppers[BITS - 1].astype(F32)
    gap_off = gap_off + jnp.where(level_of == 3 + BITS - 1, up * before + (1.0 - up) * NEVER, 0.0)
    offs[...] = gap_off
    for c in (locals_[0], locals_[3]):
        c.wait()

    owners = (y, left, right, across)

    def project(r, weights, who=owners):
        rows = pl.ds(r * BLOCK, BLOCK)
        return sum(dot(xg[i, rows, :], weights[pl.ds(pl.multiple_of(i * PART, PART), PART), :]) for i in who)

    def keys_part(r):
        rows = pl.ds(r * BLOCK, BLOCK)
        part = project(r, wkv, owners[:3])
        onward(r, 0).wait_recv()
        onward(r, 1).wait_recv()
        finish_keys(r, part + project(r, wkv, owners[3:]))

    def keys_late(r):
        rows = pl.ds((r - EARLY) * BLOCK, BLOCK)
        both = project(r, wkv, owners[:1])
        for i in range(3):
            both = both + prec[i, rows, :].astype(F32)
        finish_keys(r, both)

    def finish_keys(r, both):
        rows = pl.ds(r * BLOCK, BLOCK)
        values = both[:, SIZE:].astype(BF16)
        kb[rows, :] = both[:, :SIZE].astype(BF16)
        vb[rows, :] = values
        k_t = jnp.transpose(both[:, :SIZE].astype(BF16).astype(F32))
        weight = jnp.exp(ends[r] - dect[:, r * BLOCK : (r + 1) * BLOCK])
        for h in range(HEADS):
            scaled = (k_t * weight[h : h + 1, :]).astype(BF16)
            sb[r, h * SIZE : (h + 1) * SIZE, :] = dot(scaled, values)

    def fade_of(c, before_c, h):
        return jnp.exp(ends[c] - ends[before_c])[h : h + 1, :]

    def query_part(r):
        rows = slice(r * BLOCK, (r + 1) * BLOCK)
        qb[rows, :] = project(r, wq).astype(BF16)
        weight = softplus(sum(dot_t(xg[i, rows, :], wl_ref[:, i * PART : (i + 1) * PART]) for i in range(4)))
        kind = level_of[0:1]
        off = offs[0:1, :]
        off = jnp.where(kind == 1, -d36[r * BLOCK - 1 : r * BLOCK, :] if r % 2 else NEVER, off)
        off = jnp.where(kind == 2, -d36[2 * BLOCK - 1 : 2 * BLOCK, :] if r >= 2 else NEVER, off)
        here = d36[rows, :]
        power = jnp.where(kind == 0, 0.0, here + off)
        factor = weight * jnp.exp(power)
        keys = kb[rows, :]
        values = vb[rows, :]
        inside_row = lax.broadcasted_iota(jnp.int32, (BLOCK, BLOCK), 0)
        inside_col = lax.broadcasted_iota(jnp.int32, (BLOCK, BLOCK), 1)
        causal = inside_row >= inside_col
        along_here = dect[:, rows]
        for h in range(HEADS):
            cols = slice(h * SIZE, (h + 1) * SIZE)
            query = qb[rows, cols]
            wide = query.astype(F32)
            scores = dot_t(query, keys)
            gap = here[:, h * LEVELS : h * LEVELS + 1] - along_here[h : h + 1, :]
            mixing = jnp.exp(jnp.where(causal, gap, NEVER)) * scores * factor[:, h * LEVELS : h * LEVELS + 1]
            total = dot(mixing.astype(BF16), values)
            if r % 2:
                near_query = (wide * factor[:, h * LEVELS + 1 : h * LEVELS + 2]).astype(BF16)
                total = total + dot(near_query, sb[r - 1, cols, :].astype(BF16))
            if r >= 2:
                late_query = (wide * factor[:, h * LEVELS + 2 : h * LEVELS + 3]).astype(BF16)
                total = total + dot(late_query, sb16[cols, :])
            acc[rows, cols] = total
            for bit in range(BITS):
                at = h * LEVELS + 3 + bit
                qs[bit, rows, cols] = (wide * factor[:, at : at + 1]).astype(BF16)

    def pair_sum():
        for h in range(HEADS):
            cols = slice(h * SIZE, (h + 1) * SIZE)
            sb16[cols, :] = (sb[1, cols, :] + fade_of(1, 0, h) * sb[0, cols, :]).astype(BF16)

    keys_part(0)
    kv_share.wait_recv()
    for i in (2, 0, 1):
        psend[i] = dot(xg[y, EARLY * BLOCK :, :], wkp[i]).astype(BF16)
        kv_parts[i].start()
    over_z[1].wait_recv()

    @pl.when(jnp.logical_not(is_top))
    def _():
        pl.semaphore_wait(ready.at[0], 1)

    over_z[2].start()
    keys_part(1)
    pair_sum()
    query_part(0)
    query_part(1)
    send_own(2)
    for c in kv_parts:
        c.wait_recv()
    send_own(3)
    for r in range(EARLY, BLOCKS):
        keys_late(r)
    for h in range(HEADS):
        cols = slice(h * SIZE, (h + 1) * SIZE)
        first = sb[1, cols, :] + fade_of(1, 0, h) * sb[0, cols, :]
        second = sb[3, cols, :] + fade_of(3, 2, h) * sb[2, cols, :]
        whole = second + fade_of(3, 1, h) * first
        run[cols, :] = whole
        ssend[0, cols, :] = whole.astype(BF16)

    last_bit = BITS - 1

    def head_rows(wave):
        return pl.ds(pl.multiple_of((2 * wave + core) * SIZE, SIZE), SIZE)

    def state_copy(bit, wave):
        rows = pl.ds(2 * wave * SIZE, 2 * SIZE) if bit == 0 else head_rows(wave)
        i = 2 * bit + wave
        return remote(ssend.at[bit, rows], bkt.at[bit, rows], st_s.at[i], st_r.at[i], mates[bit])

    def top_copy(wave, device, place):
        rows = head_rows(wave)
        i = 2 * last_bit + wave
        return remote(ssend.at[last_bit, rows], bkt.at[last_bit, rows], st_s.at[i + 2 * place], st_r.at[i], device)

    def hand_over(bit, wave):
        rows = head_rows(wave)
        i = 2 * bit + wave
        return remote(bkt.at[bit, rows], bkt.at[bit, rows], fw_s.at[i], fw_r.at[i], mates[0])

    for wave in range(2):
        state_copy(0, wave).start()
    own_out.start()

    def take(bit):
        for h in range(HEADS):
            cols = slice(h * SIZE, (h + 1) * SIZE)
            acc[:, cols] += dot(qs[bit, :, cols], bkt[bit, cols, :])

    def corner(wave, third):
        rows = head_rows(wave)
        if third:
            return remote(ssend.at[1, rows], xin.at[0, rows], st_s.at[4 + wave], st_r.at[4 + wave], mates[2])
        return remote(ssend.at[1, rows], xin.at[1, rows], xs.at[wave], xr.at[wave], x_across)

    def scale(row, wave):
        return row[pl.ds(2 * wave + core, 1), :]

    def merge(bit, wave, other):
        one = head_rows(wave)
        return scale(coef.at[bit, 0], wave) * run[one, :] + scale(coef.at[bit, 1], wave) * other

    for wave in range(2):
        one = head_rows(wave)
        state_copy(0, wave).wait_recv()
        merged = merge(0, wave, bkt[0, one, :].astype(F32))
        run[one, :] = merged
        ssend[1, one, :] = merged.astype(BF16)
        corner(wave, False).start()
        state_copy(1, wave).start()
        corner(wave, True).start()
    for wave in range(2):
        one = head_rows(wave)
        state_copy(1, wave).wait_recv()
        corner(wave, True).wait_recv()
        corner(wave, False).wait_recv()
        run[one, :] = merge(1, wave, bkt[1, one, :].astype(F32))
        second = scale(pair.at[0], wave) * xin[0, one, :].astype(F32) + scale(pair.at[1], wave) * xin[1, one, :].astype(F32)
        merged = merge(2, wave, second)
        run[one, :] = merged
        ssend[3, one, :] = merged.astype(BF16)
        state_copy(3, wave).start()
        bkt[2, one, :] = second.astype(BF16)
        hand_over(1, wave).start()
        hand_over(2, wave).start()
    over_z[2].wait_recv()
    for c in over_x:
        c.start()
    pass_on(2)
    for wave in range(2):
        one = head_rows(wave)
        state_copy(3, wave).wait_recv()
        merged = merge(3, wave, bkt[3, one, :].astype(F32))
        run[one, :] = merged
        ssend[4, one, :] = merged.astype(BF16)
        state_copy(4, wave).start()
        hand_over(3, wave).start()
    pass_on(3)
    for wave in range(2):
        one = head_rows(wave)
        state_copy(4, wave).wait_recv()
        ssend[last_bit, one, :] = merge(4, wave, bkt[4, one, :].astype(F32)).astype(BF16)

        @pl.when(is_source)
        def _(wave=wave):
            if wave == 0:
                pl.semaphore_wait(ready.at[1], 2)
            top_copy(wave, near, 0).start()
            top_copy(wave, far, 1).start()

        hand_over(4, wave).start()
    for c in over_x:
        c.wait_recv()
    for c in over_x2:
        c.start()
    for r in range(2, BLOCKS):
        onward(r, 0).wait_recv()
        onward(r, 1).wait_recv()
        query_part(r)

    many = ROWS // 2

    def own_normed(u, side):
        part = ng.at[y, u // 2, pl.ds(u % 2 * many, many)]
        i = 2 * u + side
        return remote(part, part, nm_s.at[i], nm_r.at[i], to_left if side else to_right)

    def onward_normed(u, side):
        part = ng.at[right if side else left, u // 2, pl.ds(u % 2 * many + side * BLOCK, BLOCK)]
        i = 8 + 2 * u + side
        return remote(part, part, nm_s.at[i], nm_r.at[i], to_left if side else to_right)

    for wave in range(2):

        @pl.when(is_top)
        def _(wave=wave):
            top_copy(wave, source, 0).wait_recv()
            hand_over(last_bit, wave).start()

    for bit in range(last_bit):
        if bit > 0:
            for wave in range(2):
                hand_over(bit, wave).wait_recv()
        take(bit)
    for wave in range(2):

        @pl.when(is_top)
        def _(wave=wave):
            hand_over(last_bit, wave).wait_recv()

        for part in range(2):
            rows = slice(part * many, (part + 1) * many)
            for i in range(2):
                h = 2 * wave + i
                cols = slice(h * SIZE, (h + 1) * SIZE)
                value = acc[rows, cols] + dot(qs[last_bit, rows, cols], bkt[last_bit, cols, :])
                mean = jnp.mean(value * value, axis=-1, keepdims=True)
                ng[y, wave, rows, i * SIZE : (i + 1) * SIZE] = (value * lax.rsqrt(mean + 1e-05)).astype(BF16)
            own_normed(2 * wave + part, 0).start()
            own_normed(2 * wave + part, 1).start()

    def pass_normed(u):
        for side in range(2):
            own_normed(u, side).wait_recv()
            onward_normed(u, side).start()

    pass_normed(0)
    for c in over_x2:
        c.wait_recv()
    share.start()
    pass_normed(1)
    pass_normed(2)
    own_out.wait()
    share.wait_recv()

    def place(u):
        wave = u // 2
        return wave, slice(u % 2 * many, (u % 2 + 1) * many), slice(wave * 256, (wave + 1) * 256)

    for u in range(4):
        if u == 2:
            pass_normed(3)
        wave, rows, depth = place(u)
        product = dot(ng[y, wave, rows, :], wown[depth, :])
        product = product + dot(ng[left, wave, rows, :], wop[0, depth, :])
        product = product + dot(ng[right, wave, rows, :], wop[1, depth, :])
        pacc[wave, rows, :] = product
    for u in range(4):
        onward_normed(u, 0).wait_recv()
        onward_normed(u, 1).wait_recv()
        wave, rows, depth = place(u)
        product = pacc[wave, rows, :] + dot(ng[across, wave, rows, :], wop[2, depth, :])
        if wave == 0:
            pacc[0, rows, :] = product
        else:
            out_ref[rows, :] = (pacc[0, rows, :] + product).astype(BF16)

    for r in range(BLOCKS):
        for side in range(2):
            own_rows(r, side).wait_send()
            onward(r, side).wait_send()
            own_normed(r, side).wait_send()
            onward_normed(r, side).wait_send()
    for c in decay_copies + kv_fetch + kv_x + [kv_share] + kv_parts + fetch + over_z + over_x + over_x2 + [share]:
        c.wait_send()
    for wave in range(2):
        corner(wave, True).wait_send()
        corner(wave, False).wait_send()
        for bit in range(last_bit):
            if bit != 2:
                state_copy(bit, wave).wait_send()
            if bit > 0:
                hand_over(bit, wave).wait_send()

        @pl.when(is_source)
        def _(wave=wave):
            top_copy(wave, near, 0).wait_send()
            top_copy(wave, far, 1).wait_send()

        @pl.when(is_top)
        def _(wave=wave):
            hand_over(last_bit, wave).wait_send()


def body(tokens, log_decay, w_query, w_key, w_value, w_level, w_out):
    hbm = pl.BlockSpec(memory_space=pl.ANY)
    vmem = pl.BlockSpec(memory_space=pltpu.VMEM)
    dma = pltpu.SemaphoreType.DMA
    wide = HEADS * LEVELS
    return pl.pallas_call(
        kernel,
        name="layer",
        out_shape=pltpu.VMEM((ROWS, PART), BF16),
        in_specs=[hbm, vmem, hbm, hbm, hbm, vmem, hbm],
        out_specs=vmem,
        scratch_shapes=[
            pltpu.VMEM((4, ROWS, PART), BF16),
            pltpu.VMEM((4 * PART, HEADS * SIZE), BF16),
            pltpu.VMEM((4 * PART, 2 * SIZE), BF16),
            pltpu.VMEM((3, PART, 2 * SIZE), BF16),
            pltpu.VMEM((3, LATE, 2 * SIZE), BF16),
            pltpu.VMEM((3, LATE, 2 * SIZE), BF16),
            pltpu.VMEM((HEADS * SIZE, PART), BF16),
            pltpu.VMEM((3, HEADS * SIZE, PART), BF16),
            pltpu.VMEM((4, 2, ROWS, 2 * SIZE), BF16),
            pltpu.VMEM((2, ROWS, PART), F32),
            pltpu.VMEM((SIZE, ROWS), F32),
            pltpu.VMEM((ROWS, wide), F32),
            pltpu.VMEM((8, ROWS), F32),
            pltpu.VMEM((BLOCKS, 8, SIZE), F32),
            pltpu.VMEM((8, wide), F32),
            pltpu.VMEM((BITS - 1, 24, SIZE), F32),
            pltpu.VMEM((BITS - 1, 24, SIZE), F32),
            pltpu.VMEM((BITS - 1, 2, 8, SIZE), F32),
            pltpu.VMEM((2, 8, SIZE), F32),
            pltpu.VMEM((2, HEADS * SIZE, SIZE), BF16),
            pltpu.VMEM((ROWS, HEADS * SIZE), BF16),
            pltpu.VMEM((ROWS, SIZE), BF16),
            pltpu.VMEM((ROWS, SIZE), BF16),
            pltpu.VMEM((ROWS, HEADS * SIZE), F32),
            pltpu.VMEM((BITS, ROWS, HEADS * SIZE), BF16),
            pltpu.VMEM((BLOCKS, HEADS * SIZE, SIZE), F32),
            pltpu.VMEM((HEADS * SIZE, SIZE), BF16),
            pltpu.VMEM((HEADS * SIZE, SIZE), F32),
            pltpu.VMEM((BITS, HEADS * SIZE, SIZE), BF16),
            pltpu.VMEM((BITS, HEADS * SIZE, SIZE), BF16),
            dma((4 * BLOCKS,)), dma((4 * BLOCKS,)),
            dma((BITS - 1,)), dma((BITS - 1,)),
            dma((2 * BITS + 2,)), dma((2 * BITS,)),
            dma((2,)), dma((2,)),
            dma((2 * BITS,)), dma((2 * BITS,)),
            dma((12,)), dma((12,)),
            dma((10,)), dma((10,)),
            dma((4 * BLOCKS,)), dma((4 * BLOCKS,)),
            pltpu.SemaphoreType.REGULAR((2,)), dma((5,)),
        ],
        compiler_params=pltpu.CompilerParams(
            collective_id=0, has_side_effects=True, vmem_limit_bytes=56 << 20
        ),
        cost_estimate=pl.CostEstimate(flops=7_000_000_000, bytes_accessed=14_000_000, transcendentals=400_000),
    )(tokens, log_decay.T, w_query, w_key, w_value, w_level.T, w_out)


def solution(mesh):
    in_specs = (
        P("seq", "tp"),
        P("seq", "tp"),
        P(None, "tp"),
        P(None, "tp"),
        P(None, "tp"),
        P(None, "tp"),
        P("tp", None),
    )
    return jax.shard_map(
        body, mesh=mesh, in_specs=in_specs, out_specs=P("seq", "tp"), check_vma=False
    )
```
